256 devices in a mesh: seq: 32 (over z, y_lo, core), tp: 8 (over y_hi, x).
Axes of the slice: x: 4, y: 4 (y_hi: 2, y_lo: 2; y = y_hi * 2 + y_lo), z: 8, core: 2. Of those that a mesh axis runs over, the one named last changes fastest.
Arguments:
- queries: bfloat16 [16384, 8192], P('seq', 'tp'), may hold values from -6 to 6
- key_inputs: bfloat16 [16384, 8192], P('seq', 'tp'), may hold values from -6 to 6
- value_inputs: bfloat16 [16384, 8192], P('seq', 'tp'), may hold values from -6 to 6
- filters: bfloat16 [512, 128], P('tp'), may hold values from -0.5 to 0.5
- doc_ids: int32 [16384], P('seq'), may hold values from 0 to 31, never falling along the last dimension, each value on 1 to 1024 neighbouring positions
- cotangent: bfloat16 [16384, 8192], P('seq', 'tp'), may hold values from -200 to 200
Outputs:
- gated_out: bfloat16 [16384, 8192], P('seq', 'tp')
- grad_queries: bfloat16 [16384, 8192], P('seq', 'tp')
- grad_keys: bfloat16 [16384, 8192], P('seq', 'tp')
- grad_values: bfloat16 [16384, 8192], P('seq', 'tp')
- grad_filters: float32 [512, 128], P('tp')
The draws below stay inside these ranges and needn't reach their ends.
Inputs may be any that keep to these rules, and one draw needn't show every extreme that they name: `doc_ids`: documents are runs of consecutive positions numbered 0, 1, 2, ... in order of position; each has 1 to 1024 positions, and one has exactly 1024.
All inputs are finite; a program needn't handle non-finite values.
Results may differ from the reference program's by a relative error of at most 0.0053.
Values may be sent and summed in bfloat16 or wider, within the bound.
A program may use at most 64 MiB of HBM per device.

```python
import math
import jax
import jax.numpy as jnp
import numpy as np
from jax import lax

D = 8192
FILT = 128
GROUP = 16
G = 512
TOKENS = 16384
DOCS = 32
MOST = 1024


def draw_cotangent(key, part):
    key = jax.random.fold_in(key, 7)
    key_spread, key_jitter = jax.random.split(key, 2)
    spread = jax.random.uniform(key_spread, (G,), jnp.float32)
    group_trend = jnp.arange(G, dtype=jnp.float32) / max(G - 1, 1)
    row_trend = jnp.arange(TOKENS, dtype=jnp.float32) / (TOKENS - 1)
    levels = 10.0 ** (0.5 * spread + 0.5 * group_trend)
    row_scales = 3.0 ** (0.5 * row_trend)
    jitter = jax.random.normal(key_jitter, (TOKENS, D), jnp.float32)
    scales = jnp.repeat(levels, GROUP)[None, :] * row_scales[:, None]
    return (jitter * scales).astype(jnp.bfloat16)


def shard_levels(own_key, shape, shards, smallest, top_value):
    loudness = 1.0
    for dim, shards_of in shards:
        draws = jax.random.uniform(jax.random.fold_in(jax.random.fold_in(own_key, 6), dim), (shards_of,), jnp.float32, smallest / len(shards), top_value / len(shards))
        loudness = loudness * jnp.repeat(jnp.exp(draws), shape[dim] // shards_of).reshape((-1,) + (1,) * (len(shape) - 1 - dim))
    return loudness


def split_up(count, total, most, lean):
    loads = [(1 << 20) // math.isqrt(rank ** lean) + 1 for rank in range(2, count + 1)]
    rest, counts = total - most - (count - 1), [1] * (count - 1)
    while rest > 0:
        movable = [i for i in range(count - 1) if counts[i] < most]
        whole, budget = sum([loads[i] for i in movable]), rest
        for i in movable:
            addition = min(most - counts[i], max(1, budget * loads[i] // whole), rest)
            counts[i] = counts[i] + addition
            rest = rest - addition
    return np.array([most] + counts)


def ragged(stream_key, number_of, total, limit, slope):
    if number_of == 2:
        one = jax.random.randint(stream_key, (), max(1, total - limit), min(limit, total - 1) + 1)
        return jnp.stack([one, total - one])
    tallies = jnp.asarray(split_up(number_of, total, limit, slope), jnp.int32)
    twos = (number_of - 1) // 2
    donor, taker = tallies[1:1 + 2 * twos:2], tallies[2:2 + 2 * twos:2]
    slack = jnp.minimum(donor - 1, limit - taker)
    passed = jax.random.randint(jax.random.fold_in(stream_key, 1), (twos,), 0, 1 << 20) % (slack + 1)
    tallies = tallies.at[1:1 + 2 * twos:2].set(donor - passed).at[2:2 + 2 * twos:2].set(taker + passed)
    return tallies[jax.random.permutation(jax.random.fold_in(stream_key, 2), number_of)]


def gaussian(rng, shape, width, most, cuts=(), kind=jnp.bfloat16):
    level = shard_levels(rng, shape, cuts, -0.22, 0.18) if cuts else 1.0
    drawn = jax.random.normal(rng, shape, jnp.float32) * width * level
    return jnp.minimum(jnp.maximum(drawn, -most), most).astype(kind)


def setup_inputs(seed: int = 0) -> dict:
    streams_of = jax.random.split(jax.random.key(seed), 7)
    return {
        "queries": gaussian(streams_of[0], (TOKENS, D), 1.0, 6.0, ((0, 32), (1, 8))),
        "key_inputs": gaussian(streams_of[1], (TOKENS, D), 1.0, 6.0, ((0, 32), (1, 8))),
        "value_inputs": gaussian(streams_of[2], (TOKENS, D), 1.0, 6.0, ((0, 32), (1, 8))),
        "filters": gaussian(streams_of[3], (G, FILT), FILT ** -0.5, 0.5, ((0, 8),)),
        "doc_ids": jnp.searchsorted(jnp.cumsum(ragged(streams_of[4], DOCS, TOKENS, MOST, 1)), jnp.arange(TOKENS), side="right").astype(jnp.int32),
        "cotangent": draw_cotangent(jax.random.fold_in(streams_of[6], 71), 0),
    }


def band_lags(tap_count):
    row_index = jnp.arange(tap_count, dtype=jnp.int32)[:, None]
    col_index = jnp.arange(2 * tap_count, dtype=jnp.int32)[None, :]
    return (row_index + tap_count - col_index, col_index - row_index)

def diagonal_sums(pairing, tap_count):
    groups = pairing.shape[0]
    flattened = pairing.reshape(groups, tap_count * 2 * tap_count)
    flattened = jnp.pad(flattened, ((0, 0), (0, tap_count)))
    skewed = flattened.reshape(groups, tap_count, 2 * tap_count + 1)[:, :, 1:tap_count + 1]
    return lax.optimization_barrier(jnp.sum(skewed, axis=1))[:, ::-1]

def reference(queries, key_inputs, value_inputs, filters, doc_ids, cotangent):
    token_count, chan_count = queries.shape
    groups, tap_count = filters.shape
    group_size = chan_count // groups
    blocks = token_count // tap_count
    product = (key_inputs.astype(jnp.float32) * value_inputs.astype(jnp.float32)).astype(jnp.bfloat16)
    grad_z = (cotangent.astype(jnp.float32) * queries.astype(jnp.float32)).astype(jnp.bfloat16)
    lag_fwd, lag_bwd = band_lags(tap_count)
    taps_wide = filters.astype(jnp.float32)
    band_fwd = jnp.where((lag_fwd >= 0) & (lag_fwd < tap_count), taps_wide[:, jnp.clip(lag_fwd, 0, tap_count - 1)], 0.0)
    band_bwd = jnp.where((lag_bwd >= 0) & (lag_bwd < tap_count), taps_wide[:, jnp.clip(lag_bwd, 0, tap_count - 1)], 0.0)
    pad_rows = jnp.zeros((tap_count, chan_count), jnp.bfloat16)
    none_docs = jnp.full((tap_count,), -1, jnp.int32)
    prod_ext = jnp.concatenate([pad_rows, product], axis=0)
    grad_ext = jnp.concatenate([grad_z, pad_rows], axis=0)
    docs_fwd = jnp.concatenate([none_docs, doc_ids])
    docs_bwd = jnp.concatenate([doc_ids, none_docs])

    def one_block(block):
        offset = (block * tap_count).astype(jnp.int32)
        own_docs = lax.dynamic_slice_in_dim(doc_ids, offset, tap_count)
        same_fwd = (lax.dynamic_slice_in_dim(docs_fwd, offset, 2 * tap_count)[None, :] == own_docs[:, None]).astype(jnp.float32)
        same_bwd = (lax.dynamic_slice_in_dim(docs_bwd, offset, 2 * tap_count)[None, :] == own_docs[:, None]).astype(jnp.float32)
        prod_win = lax.dynamic_slice_in_dim(prod_ext, offset, 2 * tap_count, 0).astype(jnp.float32).reshape(2 * tap_count, groups, group_size)
        grad_win = lax.dynamic_slice_in_dim(grad_ext, offset, 2 * tap_count, 0).astype(jnp.float32).reshape(2 * tap_count, groups, group_size)
        conv_block = jnp.einsum('gis,sgc->igc', band_fwd * same_fwd[None], prod_win).reshape(tap_count, chan_count)
        back_block = jnp.einsum('gis,sgc->igc', band_bwd * same_bwd[None], grad_win).reshape(tap_count, chan_count)
        pairing = jnp.einsum('igc,sgc->gis', grad_win[:tap_count], prod_win) * same_fwd[None]
        return (conv_block, back_block, diagonal_sums(pairing, tap_count))
    conv_all, back_all, filt_all = lax.map(one_block, jnp.arange(blocks, dtype=jnp.int32))
    conv = conv_all.reshape(token_count, chan_count)
    grad_product = back_all.reshape(token_count, chan_count)
    filter_raw = lax.optimization_barrier(jnp.sum(filt_all, axis=0))
    gated_out = (queries.astype(jnp.float32) * conv).astype(jnp.bfloat16)
    grad_queries = (cotangent.astype(jnp.float32) * conv).astype(jnp.bfloat16)
    grad_keys = (grad_product * value_inputs.astype(jnp.float32)).astype(jnp.bfloat16)
    grad_values = (grad_product * key_inputs.astype(jnp.float32)).astype(jnp.bfloat16)
    energy = jnp.sum(filter_raw * filter_raw)
    clip_bound = 1.5 * math.sqrt(groups * tap_count * group_size * token_count)
    clip_scale = jnp.minimum(1.0, clip_bound / (jnp.sqrt(energy) + 1e-06))
    grad_filters = filter_raw * clip_scale
    return (gated_out, grad_queries, grad_keys, grad_values, grad_filters)
```

```python
import functools, math
import jax, jax.numpy as jnp
from jax import lax
from jax.experimental import pallas as pl
from jax.experimental.pallas import tpu as pltpu
from jax.sharding import PartitionSpec as P

BLK = 128
CH = 16
EXTRA = 4
F32, BF16 = jnp.float32, jnp.bfloat16

MESH = pl.DeviceIdType.MESH


def block_docs(ids_ref, blocks):
    first = [ids_ref[BLK * b] for b in range(blocks)]
    last = [ids_ref[BLK * b + BLK - 1] for b in range(blocks)]
    before = [jnp.int32(0)]
    for b in range(blocks):
        before.append(before[-1] + last[b] - first[b])
    return first, last, before


def extra_slot(first, before, blocks, e):
    b_of, doc = jnp.int32(0), first[0] + 1 + e
    for b in range(1, blocks):
        here = before[b] <= e
        b_of = jnp.where(here, b, b_of)
        doc = jnp.where(here, first[b] + 1 + e - before[b], doc)
    return b_of, doc


def main_kernel(blocks, groups,
                ids_ref, q_ref, k_ref, v_ref, c_ref, ph_ref, zh_ref, f_ref, docs_ref, ldocs_ref, rdocs_ref,
                go_ref, gq_ref, gk_ref, gv_ref, part_ref,
                pt, zt, cv, bk, rolled, folded):
    first, last, before = block_docs(ids_ref, blocks)
    total = before[blocks]
    chans = groups * CH
    step = pl.program_id(0)

    def turned(x):
        return x.T

    for b in range(blocks):
        rows = pl.ds(BLK * b, BLK)
        k, v = k_ref[rows, :].astype(F32), v_ref[rows, :].astype(F32)
        pt[b + 1] = turned((k * v).astype(BF16))
        c, q = c_ref[rows, :].astype(F32), q_ref[rows, :].astype(F32)
        zt[b] = turned((c * q).astype(BF16))
    pt[0] = turned(ph_ref[...])
    zt[blocks] = turned(zh_ref[...])

    taps = f_ref[pl.ds(pl.multiple_of(step * groups, groups), groups), :].astype(F32) if f_ref.shape[0] != groups else f_ref[...].astype(F32)
    for s in range(8):
        rolled[pl.ds(s, groups, stride=8), :] = pltpu.roll(taps, s, 1) if s else taps

    row = lax.broadcasted_iota(jnp.int32, (BLK, BLK), 0)
    lane = lax.broadcasted_iota(jnp.int32, (BLK, BLK), 1)
    upper = lane >= row

    def mask_of(docs, doc, on=None):
        m = docs == doc
        if on is not None:
            m = m & on
        return jnp.broadcast_to(m.astype(F32), (CH, BLK)).astype(BF16)

    def one_pass(start, main):
        d = [docs_ref[b:b + 1, :] for b in range(blocks)]
        if main:
            d_prev = [ldocs_ref[...]] + d[:-1]
            d_next = d[1:] + [rdocs_ref[...]]
            m_prev = [mask_of(d_prev[b], first[b]) for b in range(blocks)]
            m_cur = [mask_of(d[b], first[b]) for b in range(blocks)]
            m_last = [mask_of(d[b], last[b]) for b in range(blocks)]
            m_next = [mask_of(d_next[b], last[b]) for b in range(blocks)]
        where_, x_b, y_b, x_m, y_m = [], [], [], [], []
        for e in range(EXTRA):
            b_e, doc_e = extra_slot(first, before, blocks, start + e)
            live = start + e < total
            where_.append(b_e)
            xs = [mask_of(d[b], doc_e, live & (b_e == b)) for b in range(blocks)]
            ys = [mask_of(d[b], doc_e - 1, live & (b_e == b)) for b in range(blocks)]
            x_b.append(xs)
            y_b.append(ys)
            x_m.append(xs[0] + xs[1] + xs[2] + xs[3])
            y_m.append(ys[0] + ys[1] + ys[2] + ys[3])
        nothing = jnp.zeros((CH, BLK), BF16)
        for g in range(groups):
            rows = pl.ds(CH * g, CH)
            base = rolled[pl.ds(8 * g, 8), :]
            ring = jnp.concatenate([pltpu.roll(base, 8 * r, 1) if r else base for r in range(BLK // 8)], axis=0)
            low = jnp.where(upper, ring, 0.0).astype(BF16)
            up = jnp.where(upper, 0.0, ring).astype(BF16)
            p_left, p_here, z_here, z_right, z_pair = [], [], [], [], []
            if main:
                p = [pt[b, rows, :] for b in range(blocks + 1)]
                z = [zt[b, rows, :] for b in range(blocks + 1)]
                for b in range(blocks):
                    p_left.append(p[b] * m_prev[b])
                    p_here.append(p[b + 1] * m_cur[b])
                    z_here.append(z[b] * m_last[b])
                    z_right.append(z[b + 1] * m_next[b])
                    z_pair.append(z[b] * m_cur[b])
            for e in range(EXTRA):
                pe, ze = pt[where_[e] + 1, rows, :], zt[where_[e], rows, :]
                p_left.append(nothing)
                p_here.append(pe * x_m[e])
                z_here.append(ze * y_m[e])
                z_right.append(nothing)
                z_pair.append(ze * x_m[e])
            p_win = jnp.concatenate([jnp.concatenate(p_left, 0), jnp.concatenate(p_here, 0)], 1)
            z_win = jnp.concatenate([jnp.concatenate(z_here, 0), jnp.concatenate(z_right, 0)], 1)
            conv = jnp.dot(p_win, jnp.concatenate([up, low], 0), preferred_element_type=F32).astype(BF16)
            back = lax.dot_general(z_win, jnp.concatenate([low, up], 1), (((1,), (1,)), ((), ())),
                                   preferred_element_type=F32).astype(BF16)
            pair = jnp.dot(jnp.concatenate(z_pair, 0).T, p_win, preferred_element_type=F32)
            off = blocks if main else 0
            for b in range(blocks):
                acc = conv[CH * b:CH * b + CH] * m_cur[b] if main else cv[b, rows, :]
                acb = back[CH * b:CH * b + CH] * m_last[b] if main else bk[b, rows, :]
                for e in range(EXTRA):
                    sl = slice(CH * (off + e), CH * (off + e + 1))
                    acc = acc + conv[sl] * x_b[e][b]
                    acb = acb + back[sl] * y_b[e][b]
                cv[b, rows, :] = acc
                bk[b, rows, :] = acb
            merged = jnp.where(lane <= row, pair[:, BLK:], pair[:, :BLK])
            fold = None if main else folded[pl.ds(8 * g, 8), :]
            for r in range(BLK // 8):
                part = merged[8 * r:8 * r + 8]
                part = pltpu.roll(part, BLK - 8 * r, 1) if r else part
                fold = part if fold is None else fold + part
            folded[pl.ds(8 * g, 8), :] = fold

    one_pass(jnp.int32(0), True)

    def more(p, carry):
        one_pass(p * EXTRA, False)
        return carry

    lax.fori_loop(1, (total + EXTRA - 1) // EXTRA, more, 0)

    raw = folded[pl.ds(0, groups, stride=8), :]
    for i in range(1, 8):
        raw = raw + pltpu.roll(folded[pl.ds(i, groups, stride=8), :], BLK - i, 1)
    flip = (lane == (BLK - row) % BLK).astype(F32)
    raw = jnp.dot(raw, flip, precision=lax.Precision.HIGHEST, preferred_element_type=F32)
    for h in range(groups // 2):
        part_ref[h] = raw[2 * h:2 * h + 2]

    for b in range(blocks):
        rows = pl.ds(BLK * b, BLK)
        conv, back = cv[b].T.astype(F32), bk[b].T.astype(F32)
        go_ref[rows, :] = (q_ref[rows, :].astype(F32) * conv).astype(BF16)
        gq_ref[rows, :] = (c_ref[rows, :].astype(F32) * conv).astype(BF16)
        gk_ref[rows, :] = (v_ref[rows, :].astype(F32) * back).astype(BF16)
        gv_ref[rows, :] = (k_ref[rows, :].astype(F32) * back).astype(BF16)


def main_call(q, k, v, c, ph, zh, filters, ids, docs, ldocs, rdocs, tc=256):
    rows, chans = q.shape
    blocks = rows // BLK
    groups = tc // CH
    tile = pl.BlockSpec((rows, tc), lambda i, ids: (0, i))
    rim = pl.BlockSpec((BLK, tc), lambda i, ids: (0, i))
    whole = lambda a: pl.BlockSpec(a.shape, lambda i, ids: (0,) * a.ndim)
    nat = jax.ShapeDtypeStruct((rows, chans), BF16)
    return pl.pallas_call(
        functools.partial(main_kernel, blocks, groups),
        out_shape=(nat, nat, nat, nat, jax.ShapeDtypeStruct((chans // CH // 2, 2, BLK), F32)),
        grid_spec=pltpu.PrefetchScalarGridSpec(
            num_scalar_prefetch=1,
            grid=(chans // tc,),
            in_specs=[tile] * 4 + [rim] * 2 + [pl.BlockSpec((groups, BLK), lambda i, ids: (i, 0)), whole(docs), whole(ldocs), whole(rdocs)],
            out_specs=[tile] * 4 + [pl.BlockSpec((groups // 2, 2, BLK), lambda i, ids: (i, 0, 0))],
            scratch_shapes=[
                pltpu.VMEM((blocks + 1, tc, BLK), BF16), pltpu.VMEM((blocks + 1, tc, BLK), BF16),
                pltpu.VMEM((blocks, tc, BLK), BF16), pltpu.VMEM((blocks, tc, BLK), BF16),
                pltpu.VMEM((8 * groups, BLK), F32), pltpu.VMEM((8 * groups, BLK), F32),
            ]),
        compiler_params=pltpu.CompilerParams(vmem_limit_bytes=60 * 2**20),
        name="main",
    )(ids, q, k, v, c, ph, zh, filters, docs, ldocs, rdocs)


def halo_kernel(count, q_hbm, k_hbm, v_hbm, c_hbm, docs_ref, ph_ref, zh_ref, ld_ref, rd_ref,
                k_rim, v_rim, q_rim, c_rim, p_out, z_out, ld_in, rd_in, load_sem, send_sem, recv_sem):
    me = lax.axis_index("seq")
    right, left = lax.rem(me + 1, count), lax.rem(me + count - 1, count)
    barrier = pltpu.get_barrier_semaphore()
    for peer in (left, right):
        pl.semaphore_signal(barrier, inc=1, device_id={"seq": peer}, device_id_type=MESH)
    rows = k_hbm.shape[0]
    tail, head = pl.ds(rows - BLK, BLK), pl.ds(0, BLK)
    loads = [pltpu.make_async_copy(src.at[part], dst, load_sem.at[i]) for i, (src, part, dst) in enumerate(
        ((k_hbm, tail, k_rim), (v_hbm, tail, v_rim), (c_hbm, head, c_rim), (q_hbm, head, q_rim)))]
    for load in loads:
        load.start()

    def send(i, src, dst, peer):
        return pltpu.make_async_remote_copy(src_ref=src, dst_ref=dst, send_sem=send_sem.at[i], recv_sem=recv_sem.at[i],
                                            device_id={"seq": peer}, device_id_type=MESH)

    pl.semaphore_wait(barrier, 2)
    blocks = docs_ref.shape[0]
    sends = [send(2, docs_ref.at[pl.ds(blocks - 1, 1)], ld_in, right), send(3, docs_ref.at[pl.ds(0, 1)], rd_in, left)]
    for s in sends:
        s.start()
    loads[0].wait()
    loads[1].wait()
    p_out[...] = (k_rim[...].astype(F32) * v_rim[...].astype(F32)).astype(BF16)
    sends.append(send(0, p_out, ph_ref, right))
    sends[-1].start()
    loads[2].wait()
    loads[3].wait()
    z_out[...] = (c_rim[...].astype(F32) * q_rim[...].astype(F32)).astype(BF16)
    sends.append(send(1, z_out, zh_ref, left))
    sends[-1].start()
    for s in sends:
        s.wait()
    ld_ref[...] = jnp.where(me == 0, -1, ld_in[...])
    rd_ref[...] = jnp.where(me == count - 1, -1, rd_in[...])


def halo_call(count, q, k, v, c, docs):
    chans = q.shape[1]
    rim = pltpu.VMEM((BLK, chans), BF16)
    vm = pl.BlockSpec(memory_space=pltpu.VMEM)
    line = jax.ShapeDtypeStruct((1, BLK), jnp.int32)
    rim_out = jax.ShapeDtypeStruct((BLK, chans), BF16)
    return pl.pallas_call(
        functools.partial(halo_kernel, count),
        out_shape=(rim_out, rim_out, line, line),
        in_specs=[pl.BlockSpec(memory_space=pl.ANY)] * 4 + [vm],
        out_specs=(vm,) * 4,
        scratch_shapes=[rim] * 6 + [pltpu.VMEM((1, BLK), jnp.int32)] * 2
        + [pltpu.SemaphoreType.DMA((4,))] * 3,
        compiler_params=pltpu.CompilerParams(collective_id=0, has_side_effects=True, vmem_limit_bytes=60 * 2**20),
        name="halo",
    )(q, k, v, c, docs)


def sum_kernel(count, wide, bound, part_ref, out_ref, got, own, whole, energy, send_a, recv_a, send_b, recv_b, send_c, recv_c):
    me, tp = lax.axis_index("seq"), lax.axis_index("tp")
    barrier = pltpu.get_barrier_semaphore()

    def seq_peer(d):
        return lax.rem(me + d, count)

    def tp_peer(d):
        return lax.rem(tp + d, wide)

    def each(n, do):
        lax.fori_loop(1, n, lambda d, carry: (do(d), carry)[1], 0)

    each(count, lambda d: pl.semaphore_signal(barrier, inc=1, device_id={"seq": seq_peer(d)}, device_id_type=MESH))
    each(wide, lambda d: pl.semaphore_signal(barrier, inc=1, device_id={"tp": tp_peer(d)}, device_id_type=MESH))
    pl.semaphore_wait(barrier, count + wide - 2)

    def scatter(d):
        return pltpu.make_async_remote_copy(
            src_ref=part_ref.at[seq_peer(d)], dst_ref=got.at[d], send_sem=send_a.at[d], recv_sem=recv_a.at[d],
            device_id={"seq": seq_peer(d)}, device_id_type=MESH)

    def spread(d):
        return pltpu.make_async_remote_copy(
            src_ref=own, dst_ref=whole.at[me], send_sem=send_b.at[d], recv_sem=recv_b.at[d],
            device_id={"seq": seq_peer(d)}, device_id_type=MESH)

    def tell(d):
        return pltpu.make_async_remote_copy(
            src_ref=energy.at[0], dst_ref=energy.at[d], send_sem=send_c.at[d], recv_sem=recv_c.at[d],
            device_id={"tp": tp_peer(d)}, device_id_type=MESH)

    each(count, lambda d: scatter(d).start())
    got[0] = part_ref[me]
    each(count, lambda d: scatter(d).wait_recv())
    mine = jnp.sum(got[...], axis=0)
    own[...] = mine
    each(count, lambda d: spread(d).start())
    whole[me] = mine
    each(count, lambda d: spread(d).wait_recv())
    full = whole[...]
    squares = jnp.sum(full * full, axis=0)
    energy[0] = jnp.sum(squares, axis=0, keepdims=True)
    each(wide, lambda d: tell(d).start())
    each(wide, lambda d: tell(d).wait_recv())
    total = jnp.sum(energy[...])
    norm = jnp.sqrt(jnp.full((1, BLK), total, F32))
    factor = jnp.minimum(1.0, bound / (norm + 1e-06))
    for i in range(count):
        out_ref[2 * i:2 * i + 2, :] = whole[i] * factor
    each(count, lambda d: scatter(d).wait_send())
    each(count, lambda d: spread(d).wait_send())
    each(wide, lambda d: tell(d).wait_send())


def sum_call(count, wide, bound, part):
    vm = pl.BlockSpec(memory_space=pltpu.VMEM)
    n, per, taps = part.shape
    sems = pltpu.SemaphoreType.DMA
    return pl.pallas_call(
        functools.partial(sum_kernel, count, wide, bound),
        out_shape=jax.ShapeDtypeStruct((n * per, taps), F32),
        in_specs=[vm], out_specs=vm,
        scratch_shapes=[pltpu.VMEM((count, per, taps), F32), pltpu.VMEM((per, taps), F32), pltpu.VMEM((count, per, taps), F32),
                        pltpu.VMEM((wide, 1, taps), F32)] + [sems((count,))] * 4 + [sems((wide,))] * 2,
        compiler_params=pltpu.CompilerParams(collective_id=1, has_side_effects=True),
        name="total",
    )(part)


def local(queries, key_inputs, value_inputs, filters, doc_ids, cotangent):
    rows, chans = queries.shape
    groups, taps = filters.shape
    count, wide = lax.axis_size("seq"), lax.axis_size("tp")
    docs = doc_ids.reshape(rows // BLK, BLK)
    ph, zh, ldocs, rdocs = halo_call(count, queries, key_inputs, value_inputs, cotangent, docs)
    *grads, part = main_call(queries, key_inputs, value_inputs, cotangent, ph, zh, filters, doc_ids, docs, ldocs, rdocs)
    bound = 1.5 * math.sqrt(groups * wide * taps * (chans // groups) * rows * count)
    return (*grads, sum_call(count, wide, bound, part))


def solution(mesh):
    cells, bank = P("seq", "tp"), P("tp", None)
    return jax.shard_map(local, mesh=mesh, in_specs=(cells, cells, cells, bank, P("seq"), cells),
                         out_specs=(cells, cells, cells, cells, bank), check_vma=False)
```

```python
import functools, math
import jax, jax.numpy as jnp
from jax import lax
from jax.experimental import pallas as pl
from jax.experimental.pallas import tpu as pltpu
from jax.sharding import PartitionSpec as P

BLK = 128
CH = 16
EXTRA = 4
F32, BF16 = jnp.float32, jnp.bfloat16

MESH = pl.DeviceIdType.MESH


def block_docs(ids_ref, blocks):
    first = [ids_ref[BLK * b] for b in range(blocks)]
    last = [ids_ref[BLK * b + BLK - 1] for b in range(blocks)]
    before = [jnp.int32(0)]
    for b in range(blocks):
        before.append(before[-1] + last[b] - first[b])
    return first, last, before


def extra_slot(first, before, blocks, e):
    b_of, doc = jnp.int32(0), first[0] + 1 + e
    for b in range(1, blocks):
        here = before[b] <= e
        b_of = jnp.where(here, b, b_of)
        doc = jnp.where(here, first[b] + 1 + e - before[b], doc)
    return b_of, doc


def main_kernel(blocks, groups,
                ids_ref, q_ref, k_ref, v_ref, c_ref, ph_ref, zh_ref, f_ref, docs_ref, ldocs_ref, rdocs_ref,
                go_ref, gq_ref, gk_ref, gv_ref, part_ref,
                pt, zt, cv, bk, rolled, folded):
    first, last, before = block_docs(ids_ref, blocks)
    total = before[blocks]
    chans = groups * CH
    step = pl.program_id(0)

    def turned(x):
        return x.T

    for b in range(blocks):
        rows = pl.ds(BLK * b, BLK)
        k, v = k_ref[rows, :].astype(F32), v_ref[rows, :].astype(F32)
        pt[b + 1] = turned((k * v).astype(BF16))
        c, q = c_ref[rows, :].astype(F32), q_ref[rows, :].astype(F32)
        zt[b] = turned((c * q).astype(BF16))
    pt[0] = turned(ph_ref[...])
    zt[blocks] = turned(zh_ref[...])

    taps = f_ref[pl.ds(pl.multiple_of(step * groups, groups), groups), :].astype(F32) if f_ref.shape[0] != groups else f_ref[...].astype(F32)
    for s in range(8):
        rolled[pl.ds(s, groups, stride=8), :] = pltpu.roll(taps, s, 1) if s else taps

    row = lax.broadcasted_iota(jnp.int32, (BLK, BLK), 0)
    lane = lax.broadcasted_iota(jnp.int32, (BLK, BLK), 1)
    upper = lane >= row

    def mask_of(docs, doc, on=None):
        m = docs == doc
        if on is not None:
            m = m & on
        return jnp.broadcast_to(m.astype(F32), (CH, BLK)).astype(BF16)

    def one_pass(start, main):
        d = [docs_ref[b:b + 1, :] for b in range(blocks)]
        if main:
            d_prev = [ldocs_ref[...]] + d[:-1]
            d_next = d[1:] + [rdocs_ref[...]]
            m_prev = [mask_of(d_prev[b], first[b]) for b in range(blocks)]
            m_cur = [mask_of(d[b], first[b]) for b in range(blocks)]
            m_last = [mask_of(d[b], last[b]) for b in range(blocks)]
            m_next = [mask_of(d_next[b], last[b]) for b in range(blocks)]
        where_, x_b, y_b, x_m, y_m = [], [], [], [], []
        for e in range(EXTRA):
            b_e, doc_e = extra_slot(first, before, blocks, start + e)
            live = start + e < total
            where_.append(b_e)
            xs = [mask_of(d[b], doc_e, live & (b_e == b)) for b in range(blocks)]
            ys = [mask_of(d[b], doc_e - 1, live & (b_e == b)) for b in range(blocks)]
            x_b.append(xs)
            y_b.append(ys)
            x_m.append(xs[0] + xs[1] + xs[2] + xs[3])
            y_m.append(ys[0] + ys[1] + ys[2] + ys[3])
        nothing = jnp.zeros((CH, BLK), BF16)
        for g in range(groups):
            rows = pl.ds(CH * g, CH)
            base = rolled[pl.ds(8 * g, 8), :]
            ring = jnp.concatenate([pltpu.roll(base, 8 * r, 1) if r else base for r in range(BLK // 8)], axis=0)
            low = jnp.where(upper, ring, 0.0).astype(BF16)
            up = jnp.where(upper, 0.0, ring).astype(BF16)
            p_left, p_here, z_here, z_right, z_pair = [], [], [], [], []
            if main:
                p = [pt[b, rows, :] for b in range(blocks + 1)]
                z = [zt[b, rows, :] for b in range(blocks + 1)]
                for b in range(blocks):
                    p_left.append(p[b] * m_prev[b])
                    p_here.append(p[b + 1] * m_cur[b])
                    z_here.append(z[b] * m_last[b])
                    z_right.append(z[b + 1] * m_next[b])
                    z_pair.append(z[b] * m_cur[b])
            for e in range(EXTRA):
                pe, ze = pt[where_[e] + 1, rows, :], zt[where_[e], rows, :]
                p_left.append(nothing)
                p_here.append(pe * x_m[e])
                z_here.append(ze * y_m[e])
                z_right.append(nothing)
                z_pair.append(ze * x_m[e])
            p_win = jnp.concatenate([jnp.concatenate(p_left, 0), jnp.concatenate(p_here, 0)], 1)
            z_win = jnp.concatenate([jnp.concatenate(z_here, 0), jnp.concatenate(z_right, 0)], 1)
            conv = jnp.dot(p_win, jnp.concatenate([up, low], 0), preferred_element_type=F32).astype(BF16)
            back = lax.dot_general(z_win, jnp.concatenate([low, up], 1), (((1,), (1,)), ((), ())),
                                   preferred_element_type=F32).astype(BF16)
            pair = jnp.dot(jnp.concatenate(z_pair, 0).T, p_win, preferred_element_type=F32)
            off = blocks if main else 0
            for b in range(blocks):
                acc = conv[CH * b:CH * b + CH] * m_cur[b] if main else cv[b, rows, :]
                acb = back[CH * b:CH * b + CH] * m_last[b] if main else bk[b, rows, :]
                for e in range(EXTRA):
                    sl = slice(CH * (off + e), CH * (off + e + 1))
                    acc = acc + conv[sl] * x_b[e][b]
                    acb = acb + back[sl] * y_b[e][b]
                cv[b, rows, :] = acc
                bk[b, rows, :] = acb
            merged = jnp.where(lane <= row, pair[:, BLK:], pair[:, :BLK])
            fold = None if main else folded[pl.ds(8 * g, 8), :]
            for r in range(BLK // 8):
                part = merged[8 * r:8 * r + 8]
                part = pltpu.roll(part, BLK - 8 * r, 1) if r else part
                fold = part if fold is None else fold + part
            folded[pl.ds(8 * g, 8), :] = fold

    one_pass(jnp.int32(0), True)

    def more(p, carry):
        one_pass(p * EXTRA, False)
        return carry

    lax.fori_loop(1, (total + EXTRA - 1) // EXTRA, more, 0)

    raw = folded[pl.ds(0, groups, stride=8), :]
    for i in range(1, 8):
        raw = raw + pltpu.roll(folded[pl.ds(i, groups, stride=8), :], BLK - i, 1)
    flip = (lane == (BLK - row) % BLK).astype(F32)
    raw = jnp.dot(raw, flip, precision=lax.Precision.HIGHEST, preferred_element_type=F32)
    part_ref[...] = raw

    for b in range(blocks):
        rows = pl.ds(BLK * b, BLK)
        conv, back = cv[b].T.astype(F32), bk[b].T.astype(F32)
        go_ref[rows, :] = (q_ref[rows, :].astype(F32) * conv).astype(BF16)
        gq_ref[rows, :] = (c_ref[rows, :].astype(F32) * conv).astype(BF16)
        gk_ref[rows, :] = (v_ref[rows, :].astype(F32) * back).astype(BF16)
        gv_ref[rows, :] = (k_ref[rows, :].astype(F32) * back).astype(BF16)


def main_call(q, k, v, c, ph, zh, filters, ids, docs, ldocs, rdocs, tc=256):
    rows, chans = q.shape
    blocks = rows // BLK
    groups = tc // CH
    tile = pl.BlockSpec((rows, tc), lambda i, ids: (0, i))
    rim = pl.BlockSpec((BLK, tc), lambda i, ids: (0, i))
    whole = lambda a: pl.BlockSpec(a.shape, lambda i, ids: (0,) * a.ndim)
    nat = jax.ShapeDtypeStruct((rows, chans), BF16)
    return pl.pallas_call(
        functools.partial(main_kernel, blocks, groups),
        out_shape=(nat, nat, nat, nat, jax.ShapeDtypeStruct((chans // CH, BLK), F32)),
        grid_spec=pltpu.PrefetchScalarGridSpec(
            num_scalar_prefetch=1,
            grid=(chans // tc,),
            in_specs=[tile] * 4 + [rim] * 2 + [pl.BlockSpec((groups, BLK), lambda i, ids: (i, 0)), whole(docs), whole(ldocs), whole(rdocs)],
            out_specs=[tile] * 4 + [pl.BlockSpec((groups, BLK), lambda i, ids: (i, 0))],
            scratch_shapes=[
                pltpu.VMEM((blocks + 1, tc, BLK), BF16), pltpu.VMEM((blocks + 1, tc, BLK), BF16),
                pltpu.VMEM((blocks, tc, BLK), BF16), pltpu.VMEM((blocks, tc, BLK), BF16),
                pltpu.VMEM((8 * groups, BLK), F32), pltpu.VMEM((8 * groups, BLK), F32),
            ]),
        compiler_params=pltpu.CompilerParams(vmem_limit_bytes=60 * 2**20),
        name="main",
    )(ids, q, k, v, c, ph, zh, filters, docs, ldocs, rdocs)


def halo_kernel(count, q_hbm, k_hbm, v_hbm, c_hbm, docs_ref, ph_ref, zh_ref, ld_ref, rd_ref,
                k_rim, v_rim, q_rim, c_rim, p_out, z_out, ld_in, rd_in, load_sem, send_sem, recv_sem):
    me = lax.axis_index("seq")
    right, left = lax.rem(me + 1, count), lax.rem(me + count - 1, count)
    barrier = pltpu.get_barrier_semaphore()
    for peer in (left, right):
        pl.semaphore_signal(barrier, inc=1, device_id={"seq": peer}, device_id_type=MESH)
    rows = k_hbm.shape[0]
    tail, head = pl.ds(rows - BLK, BLK), pl.ds(0, BLK)
    loads = [pltpu.make_async_copy(src.at[part], dst, load_sem.at[i]) for i, (src, part, dst) in enumerate(
        ((k_hbm, tail, k_rim), (v_hbm, tail, v_rim), (c_hbm, head, c_rim), (q_hbm, head, q_rim)))]
    for load in loads:
        load.start()

    def send(i, src, dst, peer):
        return pltpu.make_async_remote_copy(src_ref=src, dst_ref=dst, send_sem=send_sem.at[i], recv_sem=recv_sem.at[i],
                                            device_id={"seq": peer}, device_id_type=MESH)

    pl.semaphore_wait(barrier, 2)
    blocks = docs_ref.shape[0]
    sends = [send(2, docs_ref.at[pl.ds(blocks - 1, 1)], ld_in, right), send(3, docs_ref.at[pl.ds(0, 1)], rd_in, left)]
    for s in sends:
        s.start()
    loads[0].wait()
    loads[1].wait()
    p_out[...] = (k_rim[...].astype(F32) * v_rim[...].astype(F32)).astype(BF16)
    sends.append(send(0, p_out, ph_ref, right))
    sends[-1].start()
    loads[2].wait()
    loads[3].wait()
    z_out[...] = (c_rim[...].astype(F32) * q_rim[...].astype(F32)).astype(BF16)
    sends.append(send(1, z_out, zh_ref, left))
    sends[-1].start()
    for s in sends:
        s.wait()
    ld_ref[...] = jnp.where(me == 0, -1, ld_in[...])
    rd_ref[...] = jnp.where(me == count - 1, -1, rd_in[...])


def halo_call(count, q, k, v, c, docs):
    chans = q.shape[1]
    rim = pltpu.VMEM((BLK, chans), BF16)
    vm = pl.BlockSpec(memory_space=pltpu.VMEM)
    line = jax.ShapeDtypeStruct((1, BLK), jnp.int32)
    rim_out = jax.ShapeDtypeStruct((BLK, chans), BF16)
    return pl.pallas_call(
        functools.partial(halo_kernel, count),
        out_shape=(rim_out, rim_out, line, line),
        in_specs=[pl.BlockSpec(memory_space=pl.ANY)] * 4 + [vm],
        out_specs=(vm,) * 4,
        scratch_shapes=[rim] * 6 + [pltpu.VMEM((1, BLK), jnp.int32)] * 2
        + [pltpu.SemaphoreType.DMA((4,))] * 3,
        compiler_params=pltpu.CompilerParams(collective_id=0, has_side_effects=True, vmem_limit_bytes=60 * 2**20),
        name="halo",
    )(q, k, v, c, docs)


QUAD = 4


def remote(src, dst, send_sem, recv_sem, to):
    return pltpu.make_async_remote_copy(src_ref=src, dst_ref=dst, send_sem=send_sem, recv_sem=recv_sem,
                                        device_id=to, device_id_type=MESH)


def sum_kernel(count, wide, bound, part_ref, out_ref, got, ring, whole, energy,
               send_a, recv_a, send_b, recv_b, send_c, recv_c, send_d, recv_d):
    me, tp = lax.axis_index("seq"), lax.axis_index("tp")
    tall = count // QUAD
    side, up = lax.rem(me, QUAD), me // QUAD
    slab = part_ref.shape[0] // QUAD

    def near(d):
        return {"seq": up * QUAD + lax.rem(side + d, QUAD)}

    def far(d):
        return {"seq": lax.rem(me + QUAD * d, count)}

    def across(d):
        return {"tp": lax.rem(tp + d, wide)}

    def rows(i):
        return pl.ds(pl.multiple_of(i * slab, slab), slab)

    barrier = pltpu.get_barrier_semaphore()
    for to, n in ((near, QUAD), (far, tall), (across, wide)):
        for d in range(1, n):
            pl.semaphore_signal(barrier, inc=1, device_id=to(d), device_id_type=MESH)
    pl.semaphore_wait(barrier, QUAD + tall + wide - 3)

    scatter = [remote(part_ref.at[rows(lax.rem(side + d, QUAD))], got.at[d], send_a.at[d], recv_a.at[d], near(d))
               for d in range(1, QUAD)]
    climb = [remote(ring.at[up], ring.at[up], send_b.at[d], recv_b.at[d], far(d)) for d in range(1, tall)]
    spread = [remote(whole.at[rows(side)], whole.at[rows(side)], send_c.at[d], recv_c.at[d], near(d)) for d in range(1, QUAD)]
    tell = [remote(energy.at[tp], energy.at[tp], send_d.at[d], recv_d.at[d], across(d)) for d in range(1, wide)]

    def start(copies):
        for copy in copies:
            copy.start()

    def arrive(copies):
        for copy in copies:
            copy.wait_recv()

    start(scatter)
    mine = part_ref[rows(side), :]
    arrive(scatter)
    for d in range(1, QUAD):
        mine = mine + got[d]
    ring[up] = mine
    start(climb)
    arrive(climb)
    mine = ring[0]
    for z in range(1, tall):
        mine = mine + ring[z]
    whole[rows(side), :] = mine
    start(spread)
    arrive(spread)
    full = whole[...]
    energy[tp] = jnp.sum(full * full, axis=0, keepdims=True)
    start(tell)
    arrive(tell)
    norm = jnp.sqrt(jnp.full((1, BLK), jnp.sum(energy[...]), F32))
    out_ref[...] = full * jnp.minimum(1.0, bound / (norm + 1e-06))
    for copy in scatter + climb + spread + tell:
        copy.wait_send()


def sum_call(count, wide, bound, part):
    vm = pl.BlockSpec(memory_space=pltpu.VMEM)
    slab = (part.shape[0] // QUAD, part.shape[1])
    tall = count // QUAD
    sems = [pltpu.SemaphoreType.DMA((n,)) for n in (QUAD, QUAD, tall, tall, QUAD, QUAD, wide, wide)]
    return pl.pallas_call(
        functools.partial(sum_kernel, count, wide, bound),
        out_shape=jax.ShapeDtypeStruct(part.shape, F32),
        in_specs=[vm], out_specs=vm,
        scratch_shapes=[pltpu.VMEM((QUAD, *slab), F32), pltpu.VMEM((tall, *slab), F32), pltpu.VMEM(part.shape, F32),
                        pltpu.VMEM((wide, 1, part.shape[1]), F32)] + sems,
        compiler_params=pltpu.CompilerParams(collective_id=1, has_side_effects=True),
        name="total",
    )(part)


def local(queries, key_inputs, value_inputs, filters, doc_ids, cotangent):
    rows, chans = queries.shape
    groups, taps = filters.shape
    count, wide = lax.axis_size("seq"), lax.axis_size("tp")
    docs = doc_ids.reshape(rows // BLK, BLK)
    ph, zh, ldocs, rdocs = halo_call(count, queries, key_inputs, value_inputs, cotangent, docs)
    *grads, part = main_call(queries, key_inputs, value_inputs, cotangent, ph, zh, filters, doc_ids, docs, ldocs, rdocs)
    bound = 1.5 * math.sqrt(groups * wide * taps * (chans // groups) * rows * count)
    return (*grads, sum_call(count, wide, bound, part))


def solution(mesh):
    cells, bank = P("seq", "tp"), P("tp", None)
    return jax.shard_map(local, mesh=mesh, in_specs=(cells, cells, cells, bank, P("seq"), cells),
                         out_specs=(cells, cells, cells, cells, bank), check_vma=False)
```

```python
import functools, math
import jax, jax.numpy as jnp
from jax import lax
from jax.experimental import pallas as pl
from jax.experimental.pallas import tpu as pltpu
from jax.sharding import PartitionSpec as P

BLK = 128
CH = 16
EXTRA = 4
QUAD = 4
TILE = 256
F32, BF16 = jnp.float32, jnp.bfloat16
MESH = pl.DeviceIdType.MESH


def block_docs(ids_ref, blocks):
    first = [ids_ref[BLK * b] for b in range(blocks)]
    last = [ids_ref[BLK * b + BLK - 1] for b in range(blocks)]
    before = [jnp.int32(0)]
    for b in range(blocks):
        before.append(before[-1] + last[b] - first[b])
    return first, last, before


def extra_slot(first, before, blocks, e):
    b_of, doc = jnp.int32(0), first[0] + 1 + e
    for b in range(1, blocks):
        here = before[b] <= e
        b_of = jnp.where(here, b, b_of)
        doc = jnp.where(here, first[b] + 1 + e - before[b], doc)
    return b_of, doc


def mask_of(docs, doc, on=None):
    m = docs == doc
    if on is not None:
        m = m & on
    return jnp.broadcast_to(m.astype(F32), (CH, BLK)).astype(BF16)


def extra_masks(docs, first, before, blocks, start):
    total = before[blocks]
    out = []
    for e in range(EXTRA):
        b_e, doc_e = extra_slot(first, before, blocks, start + e)
        live = start + e < total
        xs = [mask_of(docs[b], doc_e, live & (b_e == b)) for b in range(blocks)]
        ys = [mask_of(docs[b], doc_e - 1, live & (b_e == b)) for b in range(blocks)]
        out.append((b_e, xs, ys, sum(xs[1:], xs[0]), sum(ys[1:], ys[0])))
    return out


def band_of(base, upper):
    ring = jnp.concatenate([pltpu.roll(base, 8 * r, 1) if r else base for r in range(BLK // 8)], axis=0)
    return jnp.where(upper, ring, 0.0).astype(BF16), jnp.where(upper, 0.0, ring).astype(BF16)


def wide_mul(a, b):
    return (a.astype(F32) * b.astype(F32)).astype(BF16)


def remote(src, dst, send_sem, recv_sem, to):
    return pltpu.make_async_remote_copy(src_ref=src, dst_ref=dst, send_sem=send_sem, recv_sem=recv_sem,
                                        device_id=to, device_id_type=MESH)


def start(copies):
    for copy in copies:
        copy.start()


def arrive(copies):
    for copy in copies:
        copy.wait_recv()


def fused_kernel(count, wide, bound, chans, rows_n,
                 ids_ref, docs_ref, f_ref, q_hbm, k_hbm, v_hbm, c_hbm,
                 go_hbm, gq_hbm, gk_hbm, gv_hbm, sum_ref,
                 q_ref, k_ref, v_ref, c_ref, zn, pt, zt, cv, bk, o_go, o_gq, o_gk, o_gv,
                 p_out, p_in, z_out, z_in, ld_in, rd_in, rolled, folded, same, masks, part, got, ring, whole, energy,
                 rim_sem, load_sem, save_sem, halo_s, halo_r,
                 send_a, recv_a, send_b, recv_b, send_c, recv_c, send_d, recv_d):
    me, tp = lax.axis_index("seq"), lax.axis_index("tp")
    blocks, groups, tiles = rows_n // BLK, chans // CH, chans // TILE
    per = TILE // CH
    tall = count // QUAD
    side, up = lax.rem(me, QUAD), me // QUAD
    slab = groups // QUAD
    right, left = lax.rem(me + 1, count), lax.rem(me + count - 1, count)

    def near(d):
        return {"seq": up * QUAD + lax.rem(side + d, QUAD), "tp": tp}

    def far(d):
        return {"seq": lax.rem(me + QUAD * d, count), "tp": tp}

    def plane(d, e):
        return {"seq": up * QUAD + lax.rem(side + d, QUAD), "tp": lax.rem(tp + e, wide)}

    def slab_rows(i):
        return pl.ds(pl.multiple_of(i * slab, slab), slab)

    tail, head = pl.ds(rows_n - BLK, BLK), pl.ds(0, BLK)
    low_rows, high_rows = pl.ds(0, rows_n - BLK), pl.ds(BLK, rows_n - BLK)
    rims = [pltpu.make_async_copy(src.at[r], dst.at[r], rim_sem.at[i]) for i, (src, dst, r) in enumerate(
        ((k_hbm, k_ref, tail), (v_hbm, v_ref, tail), (c_hbm, c_ref, head), (q_hbm, q_ref, head)))]
    start(rims)
    rest = [pltpu.make_async_copy(src.at[r], dst.at[r], load_sem.at[i]) for i, (src, dst, r) in enumerate(
        ((k_hbm, k_ref, low_rows), (v_hbm, v_ref, low_rows), (c_hbm, c_ref, high_rows), (q_hbm, q_ref, high_rows)))]
    start(rest)

    barrier = pltpu.get_barrier_semaphore()
    others = [plane(d, e) for d in range(QUAD) for e in range(wide) if d or e]
    others += [far(d) for d in range(1, tall)]
    others += [{"seq": left, "tp": tp}, {"seq": right, "tp": tp}]
    for to in others:
        pl.semaphore_signal(barrier, inc=1, device_id=to, device_id_type=MESH)

    halo = [remote(p_out, p_in, halo_s.at[0], halo_r.at[0], {"seq": right, "tp": tp}),
            remote(docs_ref.at[pl.ds(blocks - 1, 1)], ld_in, halo_s.at[1], halo_r.at[1], {"seq": right, "tp": tp}),
            remote(z_out, z_in, halo_s.at[2], halo_r.at[2], {"seq": left, "tp": tp}),
            remote(docs_ref.at[pl.ds(0, 1)], rd_in, halo_s.at[3], halo_r.at[3], {"seq": left, "tp": tp})]
    scatter = [remote(part.at[slab_rows(lax.rem(side + d, QUAD))], got.at[d], send_a.at[d], recv_a.at[d], near(d))
               for d in range(1, QUAD)]
    climb = [remote(ring.at[up], ring.at[up], send_b.at[d], recv_b.at[d], far(d)) for d in range(1, tall)]
    spread = [remote(whole.at[slab_rows(side)], whole.at[slab_rows(side)], send_c.at[d], recv_c.at[d], near(d))
              for d in range(1, QUAD)]
    slot = side * wide + tp
    tell = [remote(energy.at[slot], energy.at[slot], send_d.at[d * wide + e], recv_d.at[d * wide + e], plane(d, e))
            for d in range(QUAD) for e in range(wide) if d or e]

    row = lax.broadcasted_iota(jnp.int32, (BLK, BLK), 0)
    lane = lax.broadcasted_iota(jnp.int32, (BLK, BLK), 1)
    upper = lane >= row
    first, last, before = block_docs(ids_ref, blocks)
    docs = [docs_ref[b:b + 1, :] for b in range(blocks)]
    across = [jnp.broadcast_to(d.astype(F32), (BLK, BLK)) for d in docs]
    down = [a.T for a in across]
    same[0] = jnp.where((lane <= row) & (down[0] == across[0]), 1.0, 0.0)
    for b in range(1, blocks):
        same[b] = jnp.where(down[b] == jnp.where(lane <= row, across[b], across[b - 1]), 1.0, 0.0)
    taps = f_ref[...].astype(F32)
    for s in range(8):
        rolled[pl.ds(s, groups, stride=8), :] = pltpu.roll(taps, s, 1) if s else taps

    for copy in rims:
        copy.wait()
    p_out[...] = wide_mul(k_ref[tail, :], v_ref[tail, :])
    z_out[...] = wide_mul(c_ref[head, :], q_ref[head, :])
    for copy in rest:
        copy.wait()

    def prepare(t, carry):
        cols = pl.ds(pl.multiple_of(t * TILE, TILE), TILE)
        for b in range(blocks):
            r = pl.ds(BLK * b, BLK)
            pt[b + 1, cols, :] = wide_mul(k_ref[r, cols], v_ref[r, cols]).T
            z = wide_mul(c_ref[r, cols], q_ref[r, cols])
            zn[r, cols] = z
            zt[b, cols, :] = z.T
        return carry

    lax.fori_loop(0, tiles, prepare, 0)
    pl.semaphore_wait(barrier, len(others))
    start(halo)

    nothing = jnp.zeros((CH, BLK), BF16)
    octet = BLK // CH

    def fold(acc):
        out = acc[:8]
        for r in range(1, BLK // 8):
            out = out + pltpu.roll(acc[8 * r:8 * r + 8], BLK - 8 * r, 1)
        return out

    def inner_pairs(t, carry):
        cols = pl.ds(pl.multiple_of(t * BLK, BLK), BLK)
        for g in range(octet):
            here = pl.ds(pl.multiple_of(t * BLK + CH * g, CH), CH)
            acc = None
            p = [pt[b, here, :] for b in range(1, blocks + 1)]
            for b in range(blocks):
                pick = jnp.concatenate([p[b - 1], p[b]], 1) if b else p[0]
                zero = jnp.concatenate([nothing, nothing], 1) if b else nothing
                pad = jnp.concatenate([zero] * g + [pick] + [zero] * (octet - 1 - g), 0)
                pair = jnp.dot(zn[pl.ds(BLK * b, BLK), cols], pad, preferred_element_type=F32)
                if b:
                    pair = jnp.where(lane <= row, pair[:, BLK:], pair[:, :BLK])
                pair = pair * same[b]
                acc = pair if acc is None else acc + pair
            folded[pl.ds(pl.multiple_of(t * BLK // 2 + 8 * g, 8), 8), :] = fold(acc)
        return carry

    lax.fori_loop(0, chans // BLK, inner_pairs, 0)

    arrive(halo)
    ldocs = jnp.where(me == 0, -1, ld_in[...])
    rdocs = jnp.where(me == count - 1, -1, rd_in[...])
    same[0] = jnp.where((lane > row) & (down[0] == jnp.broadcast_to(ldocs.astype(F32), (BLK, BLK))), 1.0, 0.0)

    def rim_pairs(t, carry):
        cols = pl.ds(pl.multiple_of(t * BLK, BLK), BLK)
        turned = p_in[:, cols].T
        pt[0, cols, :] = turned
        zt[blocks, cols, :] = z_in[:, cols].T
        for g in range(0, octet, 2):
            a, b = turned[CH * g:CH * g + CH], turned[CH * g + CH:CH * g + 2 * CH]
            zero = jnp.concatenate([nothing, nothing], 1)
            pad = jnp.concatenate([zero] * g + [jnp.concatenate([a, nothing], 1), jnp.concatenate([nothing, b], 1)]
                                  + [zero] * (octet - 2 - g), 0)
            pair = jnp.dot(zn[pl.ds(0, BLK), cols], pad, preferred_element_type=F32)
            for i in range(2):
                at = pl.ds(pl.multiple_of(t * BLK // 2 + 8 * (g + i), 8), 8)
                folded[at, :] = folded[at, :] + fold(pair[:, BLK * i:BLK * i + BLK] * same[0])
        return carry

    lax.fori_loop(0, chans // BLK, rim_pairs, 0)
    raw = folded[pl.ds(0, groups, stride=8), :]
    for i in range(1, 8):
        raw = raw + pltpu.roll(folded[pl.ds(i, groups, stride=8), :], BLK - i, 1)
    part[...] = raw
    start(scatter)

    d_prev, d_next = [ldocs] + docs[:-1], docs[1:] + [rdocs]
    m_prev = [mask_of(d_prev[b], first[b]) for b in range(blocks)]
    m_cur = [mask_of(docs[b], first[b]) for b in range(blocks)]
    m_last = [mask_of(docs[b], last[b]) for b in range(blocks)]
    m_next = [mask_of(d_next[b], last[b]) for b in range(blocks)]
    extras = extra_masks(docs, first, before, blocks, 0)
    flat = m_prev + m_cur + m_last + m_next
    for _, xs, ys, x, y in extras:
        flat += xs + ys + [x, y]
    for i, m in enumerate(flat):
        masks[i] = m

    def gates(t):
        def load(i):
            return masks[i]
        m_prev, m_cur, m_last, m_next = [[load(k * blocks + b) for b in range(blocks)] for k in range(4)]
        base_i, size = 4 * blocks, 2 * blocks + 2
        cols = pl.ds(t * TILE, TILE) if isinstance(t, int) else pl.ds(pl.multiple_of(t * TILE, TILE), TILE)
        for g in range(per):
            here = pl.ds(t * TILE + CH * g, CH) if isinstance(t, int) else pl.ds(pl.multiple_of(t * TILE + CH * g, CH), CH)
            at8 = pl.ds(t * (TILE // 2) + 8 * g, 8) if isinstance(t, int) else pl.ds(pl.multiple_of(t * (TILE // 2) + 8 * g, 8), 8)
            local = pl.ds(CH * g, CH)
            low, high = band_of(rolled[at8, :], upper)
            p = [pt[b, here, :] for b in range(blocks + 1)]
            z = [zt[b, here, :] for b in range(blocks + 1)]
            p_left = [p[b] * m_prev[b] for b in range(blocks)]
            p_here = [p[b + 1] * m_cur[b] for b in range(blocks)]
            z_here = [z[b] * m_last[b] for b in range(blocks)]
            z_right = [z[b + 1] * m_next[b] for b in range(blocks)]
            for e in range(EXTRA):
                b_e = extras[e][0]
                p_left.append(nothing)
                p_here.append(pt[b_e + 1, here, :] * load(base_i + e * size + 2 * blocks))
                z_here.append(zt[b_e, here, :] * load(base_i + e * size + 2 * blocks + 1))
                z_right.append(nothing)
            p_win = jnp.concatenate([jnp.concatenate(p_left, 0), jnp.concatenate(p_here, 0)], 1)
            z_win = jnp.concatenate([jnp.concatenate(z_here, 0), jnp.concatenate(z_right, 0)], 1)
            conv = jnp.dot(p_win, jnp.concatenate([high, low], 0), preferred_element_type=F32).astype(BF16)
            back = lax.dot_general(z_win, jnp.concatenate([low, high], 1), (((1,), (1,)), ((), ())),
                                   preferred_element_type=F32).astype(BF16)
            for b in range(blocks):
                acc = conv[CH * b:CH * b + CH] * m_cur[b]
                acb = back[CH * b:CH * b + CH] * m_last[b]
                for e in range(EXTRA):
                    sl = slice(CH * (blocks + e), CH * (blocks + e + 1))
                    acc = acc + conv[sl] * load(base_i + e * size + b)
                    acb = acb + back[sl] * load(base_i + e * size + blocks + b)
                cv[b, local, :] = acc
                bk[b, local, :] = acb
        for b in range(blocks):
            r = pl.ds(BLK * b, BLK)
            conv, back = cv[b].T.astype(F32), bk[b].T.astype(F32)
            o_go[r, cols] = (q_ref[r, cols].astype(F32) * conv).astype(BF16)
            o_gq[r, cols] = (c_ref[r, cols].astype(F32) * conv).astype(BF16)
            o_gk[r, cols] = (v_ref[r, cols].astype(F32) * back).astype(BF16)
            o_gv[r, cols] = (k_ref[r, cols].astype(F32) * back).astype(BF16)

    def saves(t):
        cols = pl.ds(t * TILE, TILE)
        return [pltpu.make_async_copy(src.at[:, cols], dst.at[:, cols], save_sem.at[t, i]) for i, (src, dst) in enumerate(
            ((o_go, go_hbm), (o_gq, gq_hbm), (o_gk, gk_hbm), (o_gv, gv_hbm)))]

    cut = tiles // 2

    def run(a, b):
        lax.fori_loop(a, b, lambda t, carry: (gates(t), carry)[1], 0)
        for t in range(a, b):
            start(saves(t))

    run(0, cut)
    arrive(scatter)
    mine = part[slab_rows(side), :]
    for d in range(1, QUAD):
        mine = mine + got[d]
    ring[up] = mine
    start(climb)
    run(cut, tiles)
    arrive(climb)
    mine = ring[0]
    for z in range(1, tall):
        mine = mine + ring[z]
    whole[slab_rows(side), :] = mine
    energy[slot] = jnp.sum(mine * mine, axis=0, keepdims=True)
    start(tell)
    start(spread)
    for t in range(tiles):
        for copy in saves(t):
            copy.wait()
    for copy in halo + scatter + climb:
        copy.wait_send()
    arrive(tell)
    arrive(spread)
    norm = jnp.sqrt(jnp.full((1, BLK), jnp.sum(energy[...]), F32))
    sum_ref[...] = whole[...] * jnp.minimum(1.0, bound / (norm + 1e-06))
    for copy in tell + spread:
        copy.wait_send()


def fused_call(count, wide, bound, q, k, v, c, filters, ids, docs):
    rows, chans = q.shape
    blocks, groups, tiles = rows // BLK, chans // CH, chans // TILE
    tall = count // QUAD
    vm, hbm = pl.BlockSpec(memory_space=pltpu.VMEM), pl.BlockSpec(memory_space=pl.ANY)
    nat = jax.ShapeDtypeStruct((rows, chans), BF16)
    dma = lambda *n: pltpu.SemaphoreType.DMA(n)
    big = pltpu.VMEM((rows, chans), BF16)
    rim = pltpu.VMEM((BLK, chans), BF16)
    line = pltpu.VMEM((1, BLK), jnp.int32)
    n_masks = 4 * blocks + EXTRA * (2 * blocks + 2)
    slab = groups // QUAD
    return pl.pallas_call(
        functools.partial(fused_kernel, count, wide, bound, chans, rows),
        out_shape=(nat, nat, nat, nat, jax.ShapeDtypeStruct((groups, BLK), F32)),
        in_specs=[pl.BlockSpec(memory_space=pltpu.SMEM), vm, vm] + [hbm] * 4,
        out_specs=(hbm,) * 4 + (vm,),
        scratch_shapes=[big] * 5 + [pltpu.VMEM((blocks + 1, chans, BLK), BF16)] * 2 + [pltpu.VMEM((blocks, TILE, BLK), BF16)] * 2
        + [big] * 4 + [rim] * 4 + [line] * 2
        + [pltpu.VMEM((8 * groups, BLK), F32)] * 2 + [pltpu.VMEM((blocks, BLK, BLK), F32), pltpu.VMEM((n_masks, CH, BLK), BF16),
           pltpu.VMEM((groups, BLK), F32), pltpu.VMEM((QUAD, slab, BLK), F32), pltpu.VMEM((tall, slab, BLK), F32),
           pltpu.VMEM((groups, BLK), F32), pltpu.VMEM((QUAD * wide, 1, BLK), F32)]
        + [dma(4), dma(4), dma(tiles, 4), dma(4), dma(4),
           dma(QUAD), dma(QUAD), dma(tall), dma(tall), dma(QUAD), dma(QUAD), dma(QUAD * wide), dma(QUAD * wide)],
        compiler_params=pltpu.CompilerParams(collective_id=0, has_side_effects=True, vmem_limit_bytes=60 * 2**20),
        cost_estimate=pl.CostEstimate(flops=2 * 10**9, bytes_accessed=8 * 2**20, transcendentals=0),
        name="fused",
    )(ids, docs, filters, q, k, v, c)


def finish_kernel(blocks, ids_ref, docs_ref, f_ref, total_ref, a_go, a_gq, a_gk, a_gv, q_hbm, k_hbm, v_hbm, c_hbm,
                  go_ref, gq_ref, gk_ref, gv_ref, sum_ref,
                  q_ref, k_ref, v_ref, c_ref, pt, zt, cv, bk, rolled, load_sem):
    step = pl.program_id(0)
    per = TILE // CH
    first, last, before = block_docs(ids_ref, blocks)
    total = before[blocks]
    row = lax.broadcasted_iota(jnp.int32, (BLK, BLK), 0)
    lane = lax.broadcasted_iota(jnp.int32, (BLK, BLK), 1)
    go_ref[...], gq_ref[...], gk_ref[...], gv_ref[...] = a_go[...], a_gq[...], a_gk[...], a_gv[...]

    @pl.when(step == 0)
    def _():
        flip = (lane == (BLK - row) % BLK).astype(F32)
        sum_ref[...] = jnp.dot(total_ref[...], flip, precision=lax.Precision.HIGHEST, preferred_element_type=F32)

    @pl.when(total > EXTRA)
    def _():
        cols = pl.ds(pl.multiple_of(step * TILE, TILE), TILE)
        loads = [pltpu.make_async_copy(src.at[:, cols], dst, load_sem.at[i]) for i, (src, dst) in enumerate(
            ((q_hbm, q_ref), (k_hbm, k_ref), (v_hbm, v_ref), (c_hbm, c_ref)))]
        for copy in loads:
            copy.start()
        for copy in loads:
            copy.wait()
        for b in range(blocks):
            r = pl.ds(BLK * b, BLK)
            pt[b] = wide_mul(k_ref[r, :], v_ref[r, :]).T
            zt[b] = wide_mul(c_ref[r, :], q_ref[r, :]).T
        cv[...] = jnp.zeros(cv.shape, BF16)
        bk[...] = jnp.zeros(bk.shape, BF16)
        taps = f_ref[...].astype(F32)
        for s in range(8):
            rolled[pl.ds(s, per, stride=8), :] = pltpu.roll(taps, s, 1) if s else taps
        docs = [docs_ref[b:b + 1, :] for b in range(blocks)]
        upper = lane >= row

        def more(p, carry):
            extras = extra_masks(docs, first, before, blocks, p * EXTRA)
            for g in range(per):
                here = pl.ds(CH * g, CH)
                low, _ = band_of(rolled[pl.ds(8 * g, 8), :], upper)
                p_here = jnp.concatenate([pt[x[0], here, :] * x[3] for x in extras], 0)
                z_here = jnp.concatenate([zt[x[0], here, :] * x[4] for x in extras], 0)
                conv = jnp.dot(p_here, low, preferred_element_type=F32).astype(BF16)
                back = lax.dot_general(z_here, low, (((1,), (1,)), ((), ())), preferred_element_type=F32).astype(BF16)
                for b in range(blocks):
                    acc, acb = cv[b, here, :], bk[b, here, :]
                    for e, x in enumerate(extras):
                        sl = slice(CH * e, CH * (e + 1))
                        acc = acc + conv[sl] * x[1][b]
                        acb = acb + back[sl] * x[2][b]
                    cv[b, here, :] = acc
                    bk[b, here, :] = acb
            return carry

        lax.fori_loop(1, (total + EXTRA - 1) // EXTRA, more, 0)
        for b in range(blocks):
            r = pl.ds(BLK * b, BLK)
            conv, back = cv[b].T.astype(F32), bk[b].T.astype(F32)
            go_ref[r, :] += (q_ref[r, :].astype(F32) * conv).astype(BF16)
            gq_ref[r, :] += (c_ref[r, :].astype(F32) * conv).astype(BF16)
            gk_ref[r, :] += (v_ref[r, :].astype(F32) * back).astype(BF16)
            gv_ref[r, :] += (k_ref[r, :].astype(F32) * back).astype(BF16)


def finish_call(grads, total, q, k, v, c, filters, ids, docs):
    rows, chans = q.shape
    blocks, per = rows // BLK, TILE // CH
    tile = pl.BlockSpec((rows, TILE), lambda i, ids: (0, i))
    whole = lambda a: pl.BlockSpec(a.shape, lambda i, ids: (0,) * a.ndim)
    hbm = pl.BlockSpec(memory_space=pl.ANY)
    nat = jax.ShapeDtypeStruct((rows, chans), BF16)
    cell = pltpu.VMEM((rows, TILE), BF16)
    turned = pltpu.VMEM((blocks, TILE, BLK), BF16)
    return pl.pallas_call(
        functools.partial(finish_kernel, blocks),
        out_shape=(nat, nat, nat, nat, jax.ShapeDtypeStruct(total.shape, F32)),
        grid_spec=pltpu.PrefetchScalarGridSpec(
            num_scalar_prefetch=1, grid=(chans // TILE,),
            in_specs=[whole(docs), pl.BlockSpec((per, BLK), lambda i, ids: (i, 0)), whole(total)] + [tile] * 4 + [hbm] * 4,
            out_specs=[tile] * 4 + [whole(total)],
            scratch_shapes=[cell] * 4 + [turned] * 4 + [pltpu.VMEM((8 * per, BLK), F32), pltpu.SemaphoreType.DMA((4,))]),
        compiler_params=pltpu.CompilerParams(vmem_limit_bytes=60 * 2**20),
        name="finish",
    )(ids, docs, filters, total, *grads, q, k, v, c)


def local(queries, key_inputs, value_inputs, filters, doc_ids, cotangent):
    rows, chans = queries.shape
    groups, taps = filters.shape
    count, wide = lax.axis_size("seq"), lax.axis_size("tp")
    docs = doc_ids.reshape(rows // BLK, BLK)
    bound = 1.5 * math.sqrt(groups * wide * taps * (chans // groups) * rows * count)
    *grads, total = fused_call(count, wide, bound, queries, key_inputs, value_inputs, cotangent, filters, doc_ids, docs)
    return finish_call(grads, total, queries, key_inputs, value_inputs, cotangent, filters, doc_ids, docs)


def solution(mesh):
    cells, bank = P("seq", "tp"), P("tp", None)
    return jax.shard_map(local, mesh=mesh, in_specs=(cells, cells, cells, bank, P("seq"), cells),
                         out_specs=(cells, cells, cells, cells, bank), check_vma=False)
```

```python
import functools, math
import jax, jax.numpy as jnp
from jax import lax
from jax.experimental import pallas as pl
from jax.experimental.pallas import tpu as pltpu
from jax.sharding import PartitionSpec as P

BLK = 128
CH = 16
EXTRA = 4
QUAD = 4
TILE = 256
FUSED_VMEM = 49 * 2**20
FINISH_VMEM = 49 * 2**20
F32, BF16 = jnp.float32, jnp.bfloat16
MESH = pl.DeviceIdType.MESH


def block_docs(ids_ref, blocks):
    first = [ids_ref[b, 0] for b in range(blocks)]
    last = [ids_ref[b, BLK - 1] for b in range(blocks)]
    before = [jnp.int32(0)]
    for b in range(blocks):
        before.append(before[-1] + last[b] - first[b])
    return first, last, before


def extra_slot(first, before, blocks, e):
    b_of, doc = jnp.int32(0), first[0] + 1 + e
    for b in range(1, blocks):
        here = before[b] <= e
        b_of = jnp.where(here, b, b_of)
        doc = jnp.where(here, first[b] + 1 + e - before[b], doc)
    return b_of, doc


def mask_of(docs, doc, on=None):
    m = docs == doc
    if on is not None:
        m = m & on
    return jnp.broadcast_to(m.astype(F32), (CH, BLK)).astype(BF16)


def extra_masks(docs, first, before, blocks, start):
    total = before[blocks]
    out = []
    for e in range(EXTRA):
        b_e, doc_e = extra_slot(first, before, blocks, start + e)
        live = start + e < total
        xs = [mask_of(docs[b], doc_e, live & (b_e == b)) for b in range(blocks)]
        ys = [mask_of(docs[b], doc_e - 1, live & (b_e == b)) for b in range(blocks)]
        out.append((b_e, xs, ys, sum(xs[1:], xs[0]), sum(ys[1:], ys[0])))
    return out


def band_of(base, upper):
    ring = jnp.concatenate([pltpu.roll(base, 8 * r, 1) if r else base for r in range(BLK // 8)], axis=0)
    return jnp.where(upper, ring, 0.0).astype(BF16), jnp.where(upper, 0.0, ring).astype(BF16)


def wide_mul(a, b):
    return (a.astype(F32) * b.astype(F32)).astype(BF16)


def remote(src, dst, send_sem, recv_sem, to):
    return pltpu.make_async_remote_copy(src_ref=src, dst_ref=dst, send_sem=send_sem, recv_sem=recv_sem,
                                        device_id=to, device_id_type=MESH)


def start(copies):
    for copy in copies:
        copy.start()


def arrive(copies):
    for copy in copies:
        copy.wait_recv()


def fused_kernel(count, wide, bound, chans, rows_n,
                 ids_ref, docs_ref, f_ref, q_hbm, k_hbm, v_hbm, c_hbm,
                 go_hbm, gq_hbm, gk_hbm, gv_hbm, sum_ref,
                 q_ref, k_ref, v_ref, c_ref, zn, pt, zt, cv, bk, o_go, o_gq, o_gk, o_gv,
                 p_out, p_in, z_out, z_in, ld_in, rd_in, rolled, folded, same, masks, part, got, ring, whole, energy,
                 rim_sem, load_sem, save_sem, halo_s, halo_r,
                 send_a, recv_a, send_b, recv_b, send_c, recv_c, send_d, recv_d):
    me, tp = lax.axis_index("seq"), lax.axis_index("tp")
    blocks, groups, tiles = rows_n // BLK, chans // CH, chans // TILE
    per = TILE // CH
    tall = count // QUAD
    side, up = lax.rem(me, QUAD), me // QUAD
    slab = groups // QUAD
    right, left = lax.rem(me + 1, count), lax.rem(me + count - 1, count)

    def near(d):
        return {"seq": up * QUAD + lax.rem(side + d, QUAD), "tp": tp}

    def far(d):
        return {"seq": lax.rem(me + QUAD * d, count), "tp": tp}

    def plane(d, e):
        return {"seq": up * QUAD + lax.rem(side + d, QUAD), "tp": lax.rem(tp + e, wide)}

    def slab_rows(i):
        return pl.ds(pl.multiple_of(i * slab, slab), slab)

    barrier = pltpu.get_barrier_semaphore()
    others = [far(d) for d in range(1, tall)]
    others += [plane(d, e) for d in range(QUAD) for e in range(wide) if d or e]
    others += [{"seq": left, "tp": tp}, {"seq": right, "tp": tp}]
    for to in others:
        pl.semaphore_signal(barrier, inc=1, device_id=to, device_id_type=MESH)

    tail, head = pl.ds(rows_n - BLK, BLK), pl.ds(0, BLK)
    low_rows, high_rows = pl.ds(0, rows_n - BLK), pl.ds(BLK, rows_n - BLK)
    rims = [pltpu.make_async_copy(src.at[r], dst.at[r], rim_sem.at[i]) for i, (src, dst, r) in enumerate(
        ((c_hbm, c_ref, head), (q_hbm, q_ref, head), (k_hbm, k_ref, tail), (v_hbm, v_ref, tail)))]
    start(rims)
    rest = [pltpu.make_async_copy(src.at[r], dst.at[r], load_sem.at[i]) for i, (src, dst, r) in enumerate(
        ((k_hbm, k_ref, low_rows), (v_hbm, v_ref, low_rows), (c_hbm, c_ref, high_rows), (q_hbm, q_ref, high_rows)))]
    start(rest)

    def tile_cols(t):
        return pl.ds(t * TILE, TILE)

    to_left, to_right = {"seq": left, "tp": tp}, {"seq": right, "tp": tp}
    halo_z = [remote(z_out.at[:, tile_cols(t)], z_in.at[:, tile_cols(t)], halo_s.at[t], halo_r.at[t], to_left) for t in range(tiles)]
    halo_d = remote(docs_ref.at[pl.ds(0, 1)], rd_in, halo_s.at[tiles], halo_r.at[tiles], to_left)
    halo_p = [remote(p_out, p_in, halo_s.at[tiles + 1], halo_r.at[tiles + 1], to_right),
              remote(docs_ref.at[pl.ds(blocks - 1, 1)], ld_in, halo_s.at[tiles + 2], halo_r.at[tiles + 2], to_right)]
    scatter = [remote(part.at[slab_rows(lax.rem(side + d, QUAD))], got.at[d], send_a.at[d], recv_a.at[d], near(d))
               for d in range(1, QUAD)]
    climb = [remote(ring.at[up], ring.at[up], send_b.at[d], recv_b.at[d], far(d)) for d in range(1, tall)]
    spread = [remote(whole.at[slab_rows(side)], whole.at[slab_rows(side)], send_c.at[d], recv_c.at[d], near(d))
              for d in range(1, QUAD)]
    slot = side * wide + tp
    tell = [remote(energy.at[slot], energy.at[slot], send_d.at[d * wide + e], recv_d.at[d * wide + e], plane(d, e))
            for d in range(QUAD) for e in range(wide) if d or e]

    row = lax.broadcasted_iota(jnp.int32, (BLK, BLK), 0)
    lane = lax.broadcasted_iota(jnp.int32, (BLK, BLK), 1)
    upper = lane >= row
    first, last, before = block_docs(ids_ref, blocks)
    docs = [docs_ref[b:b + 1, :] for b in range(blocks)]
    across = [jnp.broadcast_to(d.astype(F32), (BLK, BLK)) for d in docs]
    for b in range(blocks):
        same[b] = jnp.where((lane <= row) & (across[b].T == across[b]), 1.0, 0.0)
    taps = f_ref[0].astype(F32)
    for s in range(8):
        rolled[pl.ds(s, groups, stride=8), :] = pltpu.roll(taps, s, 1) if s else taps
    m_cur = [mask_of(docs[b], first[b]) for b in range(blocks)]
    for b in range(blocks):
        masks[blocks + b] = m_cur[b]
    for b in range(1, blocks):
        masks[b] = mask_of(docs[b - 1], first[b])

    for copy in rims[:2]:
        copy.wait()
    z_out[...] = wide_mul(c_ref[head, :], q_ref[head, :])
    for copy in rims[2:]:
        copy.wait()
    p_out[...] = wide_mul(k_ref[tail, :], v_ref[tail, :])
    for copy in rest:
        copy.wait()

    def prepare(t, carry):
        cols = pl.ds(pl.multiple_of(t * TILE, TILE), TILE)
        for b in range(blocks):
            r = pl.ds(BLK * b, BLK)
            pt[b + 1, cols, :] = wide_mul(k_ref[r, cols], v_ref[r, cols]).T
            z = wide_mul(c_ref[r, cols], q_ref[r, cols])
            zn[r, cols] = z
            zt[b, cols, :] = z.T
        return carry

    lax.fori_loop(0, tiles, prepare, 0)
    pl.semaphore_wait(barrier, len(others))
    halo_d.start()
    start(halo_z)
    start(halo_p)

    nothing = jnp.zeros((CH, BLK), BF16)
    zero = jnp.concatenate([nothing, nothing], 1)
    octet = BLK // CH

    def beside(a, b):
        return [jnp.concatenate([a, nothing], 1), jnp.concatenate([nothing, b], 1)]

    def fold(acc):
        out = acc[:8]
        for r in range(1, BLK // 8):
            out = out + pltpu.roll(acc[8 * r:8 * r + 8], BLK - 8 * r, 1)
        return out

    def spot(t, g):
        return pl.multiple_of(t * TILE + CH * g, CH), pl.multiple_of(t * (TILE // 2) + 8 * g, 8)

    def inner_pairs(t, carry):
        for g in range(0, per, 2):
            h, k = g // octet, g % octet
            cols = pl.ds(pl.multiple_of(t * TILE + BLK * h, BLK), BLK)
            here = [pl.ds(spot(t, g + i)[0], CH) for i in range(2)]
            left_z, left_p = [], []
            for i in range(2):
                for b in range(1, blocks):
                    left_z.append(zt[b, here[i], :] * masks[blocks + b])
                    p = pt[b, here[i], :] * masks[b]
                    left_p.append(jnp.concatenate([nothing, p] if i else [p, nothing], 1))
                left_z.append(nothing)
                left_p.append(zero)
            prev = jnp.dot(jnp.concatenate(left_z, 0).T, jnp.concatenate(left_p, 0), preferred_element_type=F32)
            acc = [jnp.where(lane > row, prev[:, BLK * i:BLK * i + BLK], 0.0) for i in range(2)]
            for b in range(blocks):
                pad = jnp.concatenate([zero] * k + beside(pt[b + 1, here[0], :], pt[b + 1, here[1], :])
                                      + [zero] * (octet - 2 - k), 0)
                pair = jnp.dot(zn[pl.ds(BLK * b, BLK), cols], pad, preferred_element_type=F32)
                acc = [acc[i] + pair[:, BLK * i:BLK * i + BLK] * same[b] for i in range(2)]
            for i in range(2):
                folded[pl.ds(spot(t, g + i)[1], 8), :] = fold(acc[i])
        return carry

    lax.fori_loop(0, tiles, inner_pairs, 0)

    halo_d.wait_recv()
    rdocs = jnp.where(me == count - 1, -1, rd_in[...])
    beyond = jnp.broadcast_to(rdocs.astype(F32), (BLK, BLK)).T
    same[0] = jnp.where((lane > row) & (beyond == across[blocks - 1]), 1.0, 0.0)
    for t in range(tiles):
        halo_z[t].wait_recv()
        for g in range(0, per, 2):
            h, k = g // octet, g % octet
            cols = pl.ds(t * TILE + BLK * h, BLK)
            here = [pl.ds(t * TILE + CH * (g + i), CH) for i in range(2)]
            pad = jnp.concatenate([zero] * k + beside(pt[blocks, here[0], :], pt[blocks, here[1], :])
                                  + [zero] * (octet - 2 - k), 0)
            pair = jnp.dot(z_in[:, cols], pad, preferred_element_type=F32)
            for i in range(2):
                at = pl.ds(t * (TILE // 2) + 8 * (g + i), 8)
                folded[at, :] = folded[at, :] + fold(pair[:, BLK * i:BLK * i + BLK] * same[0])
    raw = folded[pl.ds(0, groups, stride=8), :]
    for i in range(1, 8):
        raw = raw + pltpu.roll(folded[pl.ds(i, groups, stride=8), :], BLK - i, 1)
    part[...] = raw
    start(scatter)
    arrive(halo_p)
    ldocs = jnp.where(me == 0, -1, ld_in[...])

    d_prev, d_next = [ldocs] + docs[:-1], docs[1:] + [rdocs]
    m_prev = [mask_of(d_prev[0], first[0])]
    m_last = [mask_of(docs[b], last[b]) for b in range(blocks)]
    m_next = [mask_of(d_next[b], last[b]) for b in range(blocks)]
    extras = extra_masks(docs, first, before, blocks, 0)
    masks[0] = m_prev[0]
    flat = m_last + m_next
    for _, xs, ys, x, y in extras:
        flat += xs + ys + [x, y]
    for i, m in enumerate(flat):
        masks[2 * blocks + i] = m

    def gates(t):
        def load(i):
            return masks[i]
        m_prev, m_cur, m_last, m_next = [[load(k * blocks + b) for b in range(blocks)] for k in range(4)]
        base_i, size = 4 * blocks, 2 * blocks + 2
        c2 = pl.ds(pl.multiple_of(t * TILE, TILE), TILE)
        pt[0, c2, :] = p_in[:, c2].T
        zt[blocks, c2, :] = z_in[:, c2].T
        cols = pl.ds(t * TILE, TILE) if isinstance(t, int) else pl.ds(pl.multiple_of(t * TILE, TILE), TILE)
        for g in range(per):
            here = pl.ds(t * TILE + CH * g, CH) if isinstance(t, int) else pl.ds(pl.multiple_of(t * TILE + CH * g, CH), CH)
            at8 = pl.ds(t * (TILE // 2) + 8 * g, 8) if isinstance(t, int) else pl.ds(pl.multiple_of(t * (TILE // 2) + 8 * g, 8), 8)
            local = pl.ds(CH * g, CH)
            low, high = band_of(rolled[at8, :], upper)
            p = [pt[b, here, :] for b in range(blocks + 1)]
            z = [zt[b, here, :] for b in range(blocks + 1)]
            p_left = [p[b] * m_prev[b] for b in range(blocks)]
            p_here = [p[b + 1] * m_cur[b] for b in range(blocks)]
            z_here = [z[b] * m_last[b] for b in range(blocks)]
            z_right = [z[b + 1] * m_next[b] for b in range(blocks)]
            for e in range(EXTRA):
                b_e = extras[e][0]
                p_left.append(nothing)
                p_here.append(pt[b_e + 1, here, :] * load(base_i + e * size + 2 * blocks))
                z_here.append(zt[b_e, here, :] * load(base_i + e * size + 2 * blocks + 1))
                z_right.append(nothing)
            p_win = jnp.concatenate([jnp.concatenate(p_left, 0), jnp.concatenate(p_here, 0)], 1)
            z_win = jnp.concatenate([jnp.concatenate(z_here, 0), jnp.concatenate(z_right, 0)], 1)
            conv = jnp.dot(p_win, jnp.concatenate([high, low], 0), preferred_element_type=F32).astype(BF16)
            back = lax.dot_general(z_win, jnp.concatenate([low, high], 1), (((1,), (1,)), ((), ())),
                                   preferred_element_type=F32).astype(BF16)
            for b in range(blocks):
                acc = conv[CH * b:CH * b + CH] * m_cur[b]
                acb = back[CH * b:CH * b + CH] * m_last[b]
                for e in range(EXTRA):
                    sl = slice(CH * (blocks + e), CH * (blocks + e + 1))
                    acc = acc + conv[sl] * load(base_i + e * size + b)
                    acb = acb + back[sl] * load(base_i + e * size + blocks + b)
                cv[b, local, :] = acc
                bk[b, local, :] = acb
        for b in range(blocks):
            r = pl.ds(BLK * b, BLK)
            conv, back = cv[b].T.astype(F32), bk[b].T.astype(F32)
            o_go[r, cols] = (q_ref[r, cols].astype(F32) * conv).astype(BF16)
            o_gq[r, cols] = (c_ref[r, cols].astype(F32) * conv).astype(BF16)
            o_gk[r, cols] = (v_ref[r, cols].astype(F32) * back).astype(BF16)
            o_gv[r, cols] = (k_ref[r, cols].astype(F32) * back).astype(BF16)

    def saves(t):
        cols = pl.ds(t * TILE, TILE)
        return [pltpu.make_async_copy(src.at[:, cols], dst.at[:, cols], save_sem.at[t, i]) for i, (src, dst) in enumerate(
            ((o_go, go_hbm), (o_gq, gq_hbm), (o_gk, gk_hbm), (o_gv, gv_hbm)))]

    cut = tiles // 2

    def run(a, b):
        lax.fori_loop(a, b, lambda t, carry: (gates(t), carry)[1], 0)
        for t in range(a, b):
            start(saves(t))

    run(0, cut)
    arrive(scatter)
    mine = part[slab_rows(side), :]
    for d in range(1, QUAD):
        mine = mine + got[d]
    ring[up] = mine
    start(climb)
    run(cut, tiles)
    arrive(climb)
    mine = ring[0]
    for z in range(1, tall):
        mine = mine + ring[z]
    whole[slab_rows(side), :] = mine
    energy[slot] = jnp.sum(mine * mine, axis=0, keepdims=True)
    start(spread)
    start(tell)
    for t in range(tiles):
        for copy in saves(t):
            copy.wait()
    for copy in halo_z + [halo_d] + halo_p + scatter + climb:
        copy.wait_send()
    arrive(tell)
    arrive(spread)
    norm = jnp.sqrt(jnp.full((1, BLK), jnp.sum(energy[...]), F32))
    sum_ref[...] = whole[...] * jnp.minimum(1.0, bound / (norm + 1e-06))
    for copy in tell + spread:
        copy.wait_send()


def fused_call(count, wide, bound, q, k, v, c, filters, docs):
    rows, chans = q.shape
    blocks, groups, tiles = rows // BLK, chans // CH, chans // TILE
    tall = count // QUAD
    vm, anywhere = pl.BlockSpec(memory_space=pltpu.VMEM), pl.BlockSpec(memory_space=pl.ANY)
    hbm = pl.BlockSpec(memory_space=pltpu.HBM)
    nat = jax.ShapeDtypeStruct((rows, chans), BF16)
    dma = lambda *n: pltpu.SemaphoreType.DMA(n)
    big = pltpu.VMEM((rows, chans), BF16)
    rim = pltpu.VMEM((BLK, chans), BF16)
    line = pltpu.VMEM((1, BLK), jnp.int32)
    n_masks = 4 * blocks + EXTRA * (2 * blocks + 2)
    slab = groups // QUAD
    return pl.pallas_call(
        functools.partial(fused_kernel, count, wide, bound, chans, rows),
        out_shape=(nat, nat, nat, nat, jax.ShapeDtypeStruct((groups, BLK), F32)),
        in_specs=[pl.BlockSpec(memory_space=pltpu.SMEM), vm, vm] + [hbm] * 4,
        out_specs=(anywhere,) * 4 + (vm,),
        scratch_shapes=[big] * 5 + [pltpu.VMEM((blocks + 1, chans, BLK), BF16)] * 2 + [pltpu.VMEM((blocks, TILE, BLK), BF16)] * 2
        + [big] * 4 + [rim] * 4 + [line] * 2
        + [pltpu.VMEM((8 * groups, BLK), F32)] * 2 + [pltpu.VMEM((blocks, BLK, BLK), F32), pltpu.VMEM((n_masks, CH, BLK), BF16),
           pltpu.VMEM((groups, BLK), F32), pltpu.VMEM((QUAD, slab, BLK), F32), pltpu.VMEM((tall, slab, BLK), F32),
           pltpu.VMEM((groups, BLK), F32), pltpu.VMEM((QUAD * wide, 1, BLK), F32)]
        + [dma(4), dma(4), dma(tiles, 4), dma(tiles + 3), dma(tiles + 3),
           dma(QUAD), dma(QUAD), dma(tall), dma(tall), dma(QUAD), dma(QUAD), dma(QUAD * wide), dma(QUAD * wide)],
        compiler_params=pltpu.CompilerParams(collective_id=0, has_side_effects=True, vmem_limit_bytes=FUSED_VMEM),
        cost_estimate=pl.CostEstimate(flops=2 * 10**9, bytes_accessed=8 * 2**20, transcendentals=0),
        name="fused",
    )(docs, docs, filters, q, k, v, c)


def finish_kernel(blocks, tiles, ids_ref, docs_ref, f_ref, total_ref, a_go, a_gq, a_gk, a_gv, q_hbm, k_hbm, v_hbm, c_hbm,
                  go_hbm, gq_hbm, gk_hbm, gv_hbm, sum_ref,
                  q_ref, k_ref, v_ref, c_ref, go_ref, gq_ref, gk_ref, gv_ref, pt, zt, cv, bk, rolled, copy_sem, load_sem):
    per = TILE // CH
    rows = a_go.shape[0]
    half = rows // 2
    results = ((a_go, go_hbm), (a_gq, gq_hbm), (a_gk, gk_hbm), (a_gv, gv_hbm))
    copies = [pltpu.make_async_copy(src.at[pl.ds(h * half, half)], dst.at[pl.ds(h * half, half)], copy_sem.at[i, h])
              for i, (src, dst) in enumerate(results) for h in range(2)]
    for copy in copies:
        copy.start()
    first, last, before = block_docs(ids_ref, blocks)
    total = before[blocks]
    row = lax.broadcasted_iota(jnp.int32, (BLK, BLK), 0)
    lane = lax.broadcasted_iota(jnp.int32, (BLK, BLK), 1)
    flip = (lane == (BLK - row) % BLK).astype(F32)
    sum_ref[...] = jnp.dot(total_ref[...], flip, precision=lax.Precision.HIGHEST, preferred_element_type=F32)
    for copy in copies:
        copy.wait()

    def add_extras(step, carry):
        cols = pl.ds(pl.multiple_of(step * TILE, TILE), TILE)
        loads = [pltpu.make_async_copy(src.at[:, cols], dst, load_sem.at[i]) for i, (src, dst) in enumerate(
            ((q_hbm, q_ref), (k_hbm, k_ref), (v_hbm, v_ref), (c_hbm, c_ref),
             (a_go, go_ref), (a_gq, gq_ref), (a_gk, gk_ref), (a_gv, gv_ref)))]
        for copy in loads:
            copy.start()
        for copy in loads:
            copy.wait()
        for b in range(blocks):
            r = pl.ds(BLK * b, BLK)
            pt[b] = wide_mul(k_ref[r, :], v_ref[r, :]).T
            zt[b] = wide_mul(c_ref[r, :], q_ref[r, :]).T
        cv[...] = jnp.zeros(cv.shape, BF16)
        bk[...] = jnp.zeros(bk.shape, BF16)
        taps = f_ref[0, pl.ds(pl.multiple_of(step * per, per), per), :].astype(F32)
        for s in range(8):
            rolled[pl.ds(s, per, stride=8), :] = pltpu.roll(taps, s, 1) if s else taps
        docs = [docs_ref[b:b + 1, :] for b in range(blocks)]
        upper = lane >= row

        def more(p, carry):
            extras = extra_masks(docs, first, before, blocks, p * EXTRA)
            for g in range(per):
                here = pl.ds(CH * g, CH)
                low, _ = band_of(rolled[pl.ds(8 * g, 8), :], upper)
                p_here = jnp.concatenate([pt[x[0], here, :] * x[3] for x in extras], 0)
                z_here = jnp.concatenate([zt[x[0], here, :] * x[4] for x in extras], 0)
                conv = jnp.dot(p_here, low, preferred_element_type=F32).astype(BF16)
                back = lax.dot_general(z_here, low, (((1,), (1,)), ((), ())), preferred_element_type=F32).astype(BF16)
                for b in range(blocks):
                    acc, acb = cv[b, here, :], bk[b, here, :]
                    for e, x in enumerate(extras):
                        sl = slice(CH * e, CH * (e + 1))
                        acc = acc + conv[sl] * x[1][b]
                        acb = acb + back[sl] * x[2][b]
                    cv[b, here, :] = acc
                    bk[b, here, :] = acb
            return carry

        lax.fori_loop(1, (total + EXTRA - 1) // EXTRA, more, 0)
        for b in range(blocks):
            r = pl.ds(BLK * b, BLK)
            conv, back = cv[b].T.astype(F32), bk[b].T.astype(F32)
            go_ref[r, :] += (q_ref[r, :].astype(F32) * conv).astype(BF16)
            gq_ref[r, :] += (c_ref[r, :].astype(F32) * conv).astype(BF16)
            gk_ref[r, :] += (v_ref[r, :].astype(F32) * back).astype(BF16)
            gv_ref[r, :] += (k_ref[r, :].astype(F32) * back).astype(BF16)
        stores = [pltpu.make_async_copy(src, dst.at[:, cols], load_sem.at[i]) for i, (src, dst) in enumerate(
            ((go_ref, go_hbm), (gq_ref, gq_hbm), (gk_ref, gk_hbm), (gv_ref, gv_hbm)))]
        for copy in stores:
            copy.start()
        for copy in stores:
            copy.wait()
        return carry

    lax.fori_loop(0, jnp.where(total > EXTRA, tiles, 0), add_extras, 0)


def finish_call(grads, total, q, k, v, c, filters, docs):
    rows, chans = q.shape
    blocks, per = rows // BLK, TILE // CH
    vm, anywhere = pl.BlockSpec(memory_space=pltpu.VMEM), pl.BlockSpec(memory_space=pl.ANY)
    hbm = pl.BlockSpec(memory_space=pltpu.HBM)
    nat = jax.ShapeDtypeStruct((rows, chans), BF16)
    cell = pltpu.VMEM((rows, TILE), BF16)
    turned = pltpu.VMEM((blocks, TILE, BLK), BF16)
    return pl.pallas_call(
        functools.partial(finish_kernel, blocks, chans // TILE),
        out_shape=(nat, nat, nat, nat, jax.ShapeDtypeStruct(total.shape, F32)),
        in_specs=[pl.BlockSpec(memory_space=pltpu.SMEM), vm, vm, vm] + [anywhere] * 4 + [hbm] * 4,
        out_specs=(hbm,) * 4 + (vm,),
        scratch_shapes=[cell] * 8 + [turned] * 4 + [pltpu.VMEM((8 * per, BLK), F32),
                                                    pltpu.SemaphoreType.DMA((4, 2)), pltpu.SemaphoreType.DMA((8,))],
        compiler_params=pltpu.CompilerParams(vmem_limit_bytes=FINISH_VMEM),
        name="finish",
    )(docs, docs, filters, total, *grads, q, k, v, c)


def local(queries, key_inputs, value_inputs, filters, doc_ids, cotangent):
    rows, chans = queries.shape
    groups, taps = filters.shape
    count, wide = lax.axis_size("seq"), lax.axis_size("tp")
    docs = doc_ids.reshape(rows // BLK, BLK)
    bank = filters.reshape(1, groups, taps)
    bound = 1.5 * math.sqrt(groups * wide * taps * (chans // groups) * rows * count)
    *grads, total = fused_call(count, wide, bound, queries, key_inputs, value_inputs, cotangent, bank, docs)
    return finish_call(grads, total, queries, key_inputs, value_inputs, cotangent, bank, docs)


def solution(mesh):
    cells, bank = P("seq", "tp"), P("tp", None)
    return jax.shard_map(local, mesh=mesh, in_specs=(cells, cells, cells, bank, P("seq"), cells),
                         out_specs=(cells, cells, cells, cells, bank), check_vma=False)
```

```python
import functools, math
import jax, jax.numpy as jnp
from jax import lax
from jax.experimental import pallas as pl
from jax.experimental.pallas import tpu as pltpu
from jax.sharding import PartitionSpec as P

BLK = 128
CH = 16
EXTRA = 4
QUAD = 4
TILE = 256
FUSED_VMEM = 49 * 2**20
FINISH_VMEM = 49 * 2**20
F32, BF16 = jnp.float32, jnp.bfloat16
MESH = pl.DeviceIdType.MESH


def block_docs(ids_ref, blocks):
    first = [ids_ref[b, 0] for b in range(blocks)]
    last = [ids_ref[b, BLK - 1] for b in range(blocks)]
    before = [jnp.int32(0)]
    for b in range(blocks):
        before.append(before[-1] + last[b] - first[b])
    return first, last, before


def extra_slot(first, before, blocks, e):
    b_of, doc = jnp.int32(0), first[0] + 1 + e
    for b in range(1, blocks):
        here = before[b] <= e
        b_of = jnp.where(here, b, b_of)
        doc = jnp.where(here, first[b] + 1 + e - before[b], doc)
    return b_of, doc


def mask_of(docs, doc, on=None):
    m = docs == doc
    if on is not None:
        m = m & on
    return jnp.broadcast_to(m.astype(F32), (CH, BLK)).astype(BF16)


def extra_masks(docs, first, before, blocks, start):
    total = before[blocks]
    out = []
    for e in range(EXTRA):
        b_e, doc_e = extra_slot(first, before, blocks, start + e)
        live = start + e < total
        xs = [mask_of(docs[b], doc_e, live & (b_e == b)) for b in range(blocks)]
        ys = [mask_of(docs[b], doc_e - 1, live & (b_e == b)) for b in range(blocks)]
        out.append((b_e, xs, ys, sum(xs[1:], xs[0]), sum(ys[1:], ys[0])))
    return out


def band_of(base, upper):
    ring = jnp.concatenate([pltpu.roll(base, 8 * r, 1) if r else base for r in range(BLK // 8)], axis=0)
    return jnp.where(upper, ring, 0.0).astype(BF16), jnp.where(upper, 0.0, ring).astype(BF16)


def wide_mul(a, b):
    return (a.astype(F32) * b.astype(F32)).astype(BF16)


def remote(src, dst, send_sem, recv_sem, to):
    return pltpu.make_async_remote_copy(src_ref=src, dst_ref=dst, send_sem=send_sem, recv_sem=recv_sem,
                                        device_id=to, device_id_type=MESH)


def start(copies):
    for copy in copies:
        copy.start()


def arrive(copies):
    for copy in copies:
        copy.wait_recv()


def fused_kernel(count, wide, bound, chans, rows_n,
                 docs_hbm, f_hbm, q_hbm, k_hbm, v_hbm, c_hbm,
                 go_hbm, gq_hbm, gk_hbm, gv_hbm, sum_ref,
                 ids_ref, docs_ref, f_ref, q_ref, k_ref, v_ref, c_ref, zn, pt, zt, cv, bk, o_go, o_gq, o_gk, o_gv,
                 p_out, p_in, z_out, z_in, ld_in, rd_in, rolled, folded, same, masks, part, got, ring, whole, energy,
                 small_sem, rim_sem, load_sem, save_sem, halo_s, halo_r,
                 send_a, recv_a, send_b, recv_b, send_c, recv_c, send_d, recv_d):
    me, tp = lax.axis_index("seq"), lax.axis_index("tp")
    blocks, groups, tiles = rows_n // BLK, chans // CH, chans // TILE
    per = TILE // CH
    tall = count // QUAD
    side, up = lax.rem(me, QUAD), me // QUAD
    slab = groups // QUAD
    right, left = lax.rem(me + 1, count), lax.rem(me + count - 1, count)

    def near(d):
        return {"seq": up * QUAD + lax.rem(side + d, QUAD), "tp": tp}

    def far(d):
        return {"seq": lax.rem(me + QUAD * d, count), "tp": tp}

    def plane(d, e):
        return {"seq": up * QUAD + lax.rem(side + d, QUAD), "tp": lax.rem(tp + e, wide)}

    def slab_rows(i):
        return pl.ds(pl.multiple_of(i * slab, slab), slab)

    barrier = pltpu.get_barrier_semaphore()
    others = [far(d) for d in range(1, tall)]
    others += [plane(d, e) for d in range(QUAD) for e in range(wide) if d or e]
    others += [{"seq": left, "tp": tp}, {"seq": right, "tp": tp}]
    for to in others:
        pl.semaphore_signal(barrier, inc=1, device_id=to, device_id_type=MESH)

    small = [pltpu.make_async_copy(src, dst, small_sem.at[i]) for i, (src, dst) in enumerate(
        ((docs_hbm, ids_ref), (docs_hbm, docs_ref), (f_hbm, f_ref)))]
    tail, head = pl.ds(rows_n - BLK, BLK), pl.ds(0, BLK)
    low_rows, high_rows = pl.ds(0, rows_n - BLK), pl.ds(BLK, rows_n - BLK)
    rims = [pltpu.make_async_copy(src.at[r], dst.at[r], rim_sem.at[i]) for i, (src, dst, r) in enumerate(
        ((c_hbm, c_ref, head), (q_hbm, q_ref, head), (k_hbm, k_ref, tail), (v_hbm, v_ref, tail)))]
    start(rims[:2])
    start(small)
    start(rims[2:])
    rest = [pltpu.make_async_copy(src.at[r], dst.at[r], load_sem.at[i]) for i, (src, dst, r) in enumerate(
        ((k_hbm, k_ref, low_rows), (v_hbm, v_ref, low_rows), (c_hbm, c_ref, high_rows), (q_hbm, q_ref, high_rows)))]
    start(rest)

    def tile_cols(t):
        return pl.ds(t * TILE, TILE)

    to_left, to_right = {"seq": left, "tp": tp}, {"seq": right, "tp": tp}
    halo_z = [remote(z_out.at[:, tile_cols(t)], z_in.at[:, tile_cols(t)], halo_s.at[t], halo_r.at[t], to_left) for t in range(tiles)]
    halo_d = remote(docs_ref.at[pl.ds(0, 1)], rd_in, halo_s.at[tiles], halo_r.at[tiles], to_left)
    halo_p = [remote(p_out, p_in, halo_s.at[tiles + 1], halo_r.at[tiles + 1], to_right),
              remote(docs_ref.at[pl.ds(blocks - 1, 1)], ld_in, halo_s.at[tiles + 2], halo_r.at[tiles + 2], to_right)]
    scatter = [remote(part.at[slab_rows(lax.rem(side + d, QUAD))], got.at[d], send_a.at[d], recv_a.at[d], near(d))
               for d in range(1, QUAD)]
    climb = [remote(ring.at[up], ring.at[up], send_b.at[d], recv_b.at[d], far(d)) for d in range(1, tall)]
    spread = [remote(whole.at[slab_rows(side)], whole.at[slab_rows(side)], send_c.at[d], recv_c.at[d], near(d))
              for d in range(1, QUAD)]
    slot = side * wide + tp
    tell = [remote(energy.at[slot], energy.at[slot], send_d.at[d * wide + e], recv_d.at[d * wide + e], plane(d, e))
            for d in range(QUAD) for e in range(wide) if d or e]

    row = lax.broadcasted_iota(jnp.int32, (BLK, BLK), 0)
    lane = lax.broadcasted_iota(jnp.int32, (BLK, BLK), 1)
    upper = lane >= row
    for copy in small:
        copy.wait()
    first, last, before = block_docs(ids_ref, blocks)
    docs = [docs_ref[b:b + 1, :] for b in range(blocks)]
    across = [jnp.broadcast_to(d.astype(F32), (BLK, BLK)) for d in docs]
    for b in range(blocks):
        same[b] = jnp.where((lane <= row) & (across[b].T == across[b]), 1.0, 0.0)
    taps = f_ref[0].astype(F32)
    for s in range(8):
        rolled[pl.ds(s, groups, stride=8), :] = pltpu.roll(taps, s, 1) if s else taps
    m_cur = [mask_of(docs[b], first[b]) for b in range(blocks)]
    for b in range(blocks):
        masks[blocks + b] = m_cur[b]
    for b in range(1, blocks):
        masks[b] = mask_of(docs[b - 1], first[b])

    for copy in rims[:2]:
        copy.wait()
    z_out[...] = wide_mul(c_ref[head, :], q_ref[head, :])
    for copy in rims[2:]:
        copy.wait()
    p_out[...] = wide_mul(k_ref[tail, :], v_ref[tail, :])
    for copy in rest:
        copy.wait()

    def prepare(t, carry):
        cols = pl.ds(pl.multiple_of(t * TILE, TILE), TILE)
        for b in range(blocks):
            r = pl.ds(BLK * b, BLK)
            pt[b + 1, cols, :] = wide_mul(k_ref[r, cols], v_ref[r, cols]).T
            z = wide_mul(c_ref[r, cols], q_ref[r, cols])
            zn[r, cols] = z
            zt[b, cols, :] = z.T
        return carry

    lax.fori_loop(0, tiles, prepare, 0)
    pl.semaphore_wait(barrier, len(others))
    halo_d.start()
    start(halo_z)

    nothing = jnp.zeros((CH, BLK), BF16)
    zero = jnp.concatenate([nothing, nothing], 1)
    octet = BLK // CH

    def beside(a, b):
        return [jnp.concatenate([a, nothing], 1), jnp.concatenate([nothing, b], 1)]

    def fold(acc):
        out = acc[:8]
        for r in range(1, BLK // 8):
            out = out + pltpu.roll(acc[8 * r:8 * r + 8], BLK - 8 * r, 1)
        return out

    def spot(t, g):
        return pl.multiple_of(t * TILE + CH * g, CH), pl.multiple_of(t * (TILE // 2) + 8 * g, 8)

    def inner_pairs(t, carry):
        for g in range(0, per, 2):
            h, k = g // octet, g % octet
            cols = pl.ds(pl.multiple_of(t * TILE + BLK * h, BLK), BLK)
            here = [pl.ds(spot(t, g + i)[0], CH) for i in range(2)]
            left_z, left_p = [], []
            for i in range(2):
                for b in range(1, blocks):
                    left_z.append(zt[b, here[i], :] * masks[blocks + b])
                    p = pt[b, here[i], :] * masks[b]
                    left_p.append(jnp.concatenate([nothing, p] if i else [p, nothing], 1))
                left_z.append(nothing)
                left_p.append(zero)
            prev = jnp.dot(jnp.concatenate(left_z, 0).T, jnp.concatenate(left_p, 0), preferred_element_type=F32)
            acc = [jnp.where(lane > row, prev[:, BLK * i:BLK * i + BLK], 0.0) for i in range(2)]
            for b in range(blocks):
                pad = jnp.concatenate([zero] * k + beside(pt[b + 1, here[0], :], pt[b + 1, here[1], :])
                                      + [zero] * (octet - 2 - k), 0)
                pair = jnp.dot(zn[pl.ds(BLK * b, BLK), cols], pad, preferred_element_type=F32)
                acc = [acc[i] + pair[:, BLK * i:BLK * i + BLK] * same[b] for i in range(2)]
            for i in range(2):
                folded[pl.ds(spot(t, g + i)[1], 8), :] = fold(acc[i])
        return carry

    lax.fori_loop(0, tiles, inner_pairs, 0)
    start(halo_p)

    halo_d.wait_recv()
    rdocs = jnp.where(me == count - 1, -1, rd_in[...])
    beyond = jnp.broadcast_to(rdocs.astype(F32), (BLK, BLK)).T
    same[0] = jnp.where((lane > row) & (beyond == across[blocks - 1]), 1.0, 0.0)
    for t in range(tiles):
        halo_z[t].wait_recv()
        for g in range(0, per, 2):
            h, k = g // octet, g % octet
            cols = pl.ds(t * TILE + BLK * h, BLK)
            here = [pl.ds(t * TILE + CH * (g + i), CH) for i in range(2)]
            pad = jnp.concatenate([zero] * k + beside(pt[blocks, here[0], :], pt[blocks, here[1], :])
                                  + [zero] * (octet - 2 - k), 0)
            pair = jnp.dot(z_in[:, cols], pad, preferred_element_type=F32)
            for i in range(2):
                at = pl.ds(t * (TILE // 2) + 8 * (g + i), 8)
                folded[at, :] = folded[at, :] + fold(pair[:, BLK * i:BLK * i + BLK] * same[0])
    raw = folded[pl.ds(0, groups, stride=8), :]
    for i in range(1, 8):
        raw = raw + pltpu.roll(folded[pl.ds(i, groups, stride=8), :], BLK - i, 1)
    part[...] = raw
    start(scatter)

    d_next = docs[1:] + [rdocs]
    m_last = [mask_of(docs[b], last[b]) for b in range(blocks)]
    m_next = [mask_of(d_next[b], last[b]) for b in range(blocks)]
    extras = extra_masks(docs, first, before, blocks, 0)
    flat = m_last + m_next
    for _, xs, ys, x, y in extras:
        flat += xs + ys + [x, y]
    for i, m in enumerate(flat):
        masks[2 * blocks + i] = m

    def gates(t):
        def load(i):
            return masks[i]
        m_prev, m_cur, m_last, m_next = [[load(k * blocks + b) for b in range(blocks)] for k in range(4)]
        base_i, size = 4 * blocks, 2 * blocks + 2
        c2 = pl.ds(pl.multiple_of(t * TILE, TILE), TILE)
        pt[0, c2, :] = p_in[:, c2].T
        zt[blocks, c2, :] = z_in[:, c2].T
        cols = pl.ds(t * TILE, TILE) if isinstance(t, int) else pl.ds(pl.multiple_of(t * TILE, TILE), TILE)
        for g in range(per):
            here = pl.ds(t * TILE + CH * g, CH) if isinstance(t, int) else pl.ds(pl.multiple_of(t * TILE + CH * g, CH), CH)
            at8 = pl.ds(t * (TILE // 2) + 8 * g, 8) if isinstance(t, int) else pl.ds(pl.multiple_of(t * (TILE // 2) + 8 * g, 8), 8)
            local = pl.ds(CH * g, CH)
            low, high = band_of(rolled[at8, :], upper)
            p = [pt[b, here, :] for b in range(blocks + 1)]
            z = [zt[b, here, :] for b in range(blocks + 1)]
            p_left = [p[b] * m_prev[b] for b in range(blocks)]
            p_here = [p[b + 1] * m_cur[b] for b in range(blocks)]
            z_here = [z[b] * m_last[b] for b in range(blocks)]
            z_right = [z[b + 1] * m_next[b] for b in range(blocks)]
            for e in range(EXTRA):
                b_e = extras[e][0]
                p_left.append(nothing)
                p_here.append(pt[b_e + 1, here, :] * load(base_i + e * size + 2 * blocks))
                z_here.append(zt[b_e, here, :] * load(base_i + e * size + 2 * blocks + 1))
                z_right.append(nothing)
            p_win = jnp.concatenate([jnp.concatenate(p_left, 0), jnp.concatenate(p_here, 0)], 1)
            z_win = jnp.concatenate([jnp.concatenate(z_here, 0), jnp.concatenate(z_right, 0)], 1)
            conv = jnp.dot(p_win, jnp.concatenate([high, low], 0), preferred_element_type=F32).astype(BF16)
            back = lax.dot_general(z_win, jnp.concatenate([low, high], 1), (((1,), (1,)), ((), ())),
                                   preferred_element_type=F32).astype(BF16)
            for b in range(blocks):
                acc = conv[CH * b:CH * b + CH] * m_cur[b]
                acb = back[CH * b:CH * b + CH] * m_last[b]
                for e in range(EXTRA):
                    sl = slice(CH * (blocks + e), CH * (blocks + e + 1))
                    acc = acc + conv[sl] * load(base_i + e * size + b)
                    acb = acb + back[sl] * load(base_i + e * size + blocks + b)
                cv[b, local, :] = acc
                bk[b, local, :] = acb
        for b in range(blocks):
            r = pl.ds(BLK * b, BLK)
            conv, back = cv[b].T.astype(F32), bk[b].T.astype(F32)
            o_go[r, cols] = (q_ref[r, cols].astype(F32) * conv).astype(BF16)
            o_gq[r, cols] = (c_ref[r, cols].astype(F32) * conv).astype(BF16)
            o_gk[r, cols] = (v_ref[r, cols].astype(F32) * back).astype(BF16)
            o_gv[r, cols] = (k_ref[r, cols].astype(F32) * back).astype(BF16)

    def saves(t):
        cols = pl.ds(t * TILE, TILE)
        return [pltpu.make_async_copy(src.at[:, cols], dst.at[:, cols], save_sem.at[t, i]) for i, (src, dst) in enumerate(
            ((o_go, go_hbm), (o_gq, gq_hbm), (o_gk, gk_hbm), (o_gv, gv_hbm)))]

    cut = tiles // 2

    def run(a, b):
        lax.fori_loop(a, b, lambda t, carry: (gates(t), carry)[1], 0)
        for t in range(a, b):
            start(saves(t))

    arrive(scatter)
    mine = part[slab_rows(side), :]
    for d in range(1, QUAD):
        mine = mine + got[d]
    ring[up] = mine
    start(climb)
    arrive(halo_p)
    masks[0] = mask_of(jnp.where(me == 0, -1, ld_in[...]), first[0])
    run(0, cut)
    arrive(climb)
    mine = ring[0]
    for z in range(1, tall):
        mine = mine + ring[z]
    whole[slab_rows(side), :] = mine
    energy[slot] = jnp.sum(mine * mine, axis=0, keepdims=True)
    start(spread)
    start(tell)
    run(cut, tiles)
    for t in range(tiles):
        for copy in saves(t):
            copy.wait()
    for copy in halo_z + [halo_d] + halo_p + scatter + climb:
        copy.wait_send()
    arrive(tell)
    arrive(spread)
    norm = jnp.sqrt(jnp.full((1, BLK), jnp.sum(energy[...]), F32))
    sum_ref[...] = whole[...] * jnp.minimum(1.0, bound / (norm + 1e-06))
    for copy in tell + spread:
        copy.wait_send()


def fused_call(count, wide, bound, q, k, v, c, filters, docs):
    rows, chans = q.shape
    blocks, groups, tiles = rows // BLK, chans // CH, chans // TILE
    tall = count // QUAD
    vm, anywhere = pl.BlockSpec(memory_space=pltpu.VMEM), pl.BlockSpec(memory_space=pl.ANY)
    hbm = pl.BlockSpec(memory_space=pltpu.HBM)
    nat = jax.ShapeDtypeStruct((rows, chans), BF16)
    dma = lambda *n: pltpu.SemaphoreType.DMA(n)
    big = pltpu.VMEM((rows, chans), BF16)
    rim = pltpu.VMEM((BLK, chans), BF16)
    line = pltpu.VMEM((1, BLK), jnp.int32)
    n_masks = 4 * blocks + EXTRA * (2 * blocks + 2)
    slab = groups // QUAD
    return pl.pallas_call(
        functools.partial(fused_kernel, count, wide, bound, chans, rows),
        out_shape=(nat, nat, nat, nat, jax.ShapeDtypeStruct((groups, BLK), F32)),
        in_specs=[anywhere] * 2 + [hbm] * 4,
        out_specs=(anywhere,) * 4 + (vm,),
        scratch_shapes=[pltpu.SMEM(docs.shape, jnp.int32), pltpu.VMEM(docs.shape, jnp.int32), pltpu.VMEM(filters.shape, BF16)]
        + [big] * 5 + [pltpu.VMEM((blocks + 1, chans, BLK), BF16)] * 2 + [pltpu.VMEM((blocks, TILE, BLK), BF16)] * 2
        + [big] * 4 + [rim] * 4 + [line] * 2
        + [pltpu.VMEM((8 * groups, BLK), F32)] * 2 + [pltpu.VMEM((blocks, BLK, BLK), F32), pltpu.VMEM((n_masks, CH, BLK), BF16),
           pltpu.VMEM((groups, BLK), F32), pltpu.VMEM((QUAD, slab, BLK), F32), pltpu.VMEM((tall, slab, BLK), F32),
           pltpu.VMEM((groups, BLK), F32), pltpu.VMEM((QUAD * wide, 1, BLK), F32)]
        + [dma(3), dma(4), dma(4), dma(tiles, 4), dma(tiles + 3), dma(tiles + 3),
           dma(QUAD), dma(QUAD), dma(tall), dma(tall), dma(QUAD), dma(QUAD), dma(QUAD * wide), dma(QUAD * wide)],
        compiler_params=pltpu.CompilerParams(collective_id=0, has_side_effects=True, vmem_limit_bytes=FUSED_VMEM),
        cost_estimate=pl.CostEstimate(flops=2 * 10**9, bytes_accessed=8 * 2**20, transcendentals=0),
        name="fused",
    )(docs, filters, q, k, v, c)


def finish_kernel(blocks, tiles, docs_hbm, f_hbm, total_hbm, a_go, a_gq, a_gk, a_gv, q_hbm, k_hbm, v_hbm, c_hbm,
                  go_hbm, gq_hbm, gk_hbm, gv_hbm, sum_hbm,
                  ids_ref, docs_ref, f_ref, total_ref, sum_ref, small_sem, q_ref, k_ref, v_ref, c_ref, go_ref, gq_ref, gk_ref, gv_ref, pt, zt, cv, bk, rolled, copy_sem, load_sem):
    per = TILE // CH
    rows = a_go.shape[0]
    half = rows // 2
    results = ((a_go, go_hbm), (a_gq, gq_hbm), (a_gk, gk_hbm), (a_gv, gv_hbm))
    copies = [pltpu.make_async_copy(src.at[pl.ds(h * half, half)], dst.at[pl.ds(h * half, half)], copy_sem.at[i, h])
              for i, (src, dst) in enumerate(results) for h in range(2)]
    for copy in copies:
        copy.start()
    small = [pltpu.make_async_copy(src, dst, small_sem.at[i]) for i, (src, dst) in enumerate(
        ((total_hbm, total_ref), (docs_hbm, ids_ref), (docs_hbm, docs_ref), (f_hbm, f_ref)))]
    start(small)
    row = lax.broadcasted_iota(jnp.int32, (BLK, BLK), 0)
    lane = lax.broadcasted_iota(jnp.int32, (BLK, BLK), 1)
    flip = (lane == (BLK - row) % BLK).astype(F32)
    small[0].wait()
    sum_ref[...] = jnp.dot(total_ref[...], flip, precision=lax.Precision.HIGHEST, preferred_element_type=F32)
    save = pltpu.make_async_copy(sum_ref, sum_hbm, small_sem.at[4])
    save.start()
    for copy in small[1:]:
        copy.wait()
    first, last, before = block_docs(ids_ref, blocks)
    total = before[blocks]
    save.wait()
    for copy in copies:
        copy.wait()

    def add_extras(step, carry):
        cols = pl.ds(pl.multiple_of(step * TILE, TILE), TILE)
        loads = [pltpu.make_async_copy(src.at[:, cols], dst, load_sem.at[i]) for i, (src, dst) in enumerate(
            ((q_hbm, q_ref), (k_hbm, k_ref), (v_hbm, v_ref), (c_hbm, c_ref),
             (a_go, go_ref), (a_gq, gq_ref), (a_gk, gk_ref), (a_gv, gv_ref)))]
        for copy in loads:
            copy.start()
        for copy in loads:
            copy.wait()
        for b in range(blocks):
            r = pl.ds(BLK * b, BLK)
            pt[b] = wide_mul(k_ref[r, :], v_ref[r, :]).T
            zt[b] = wide_mul(c_ref[r, :], q_ref[r, :]).T
        cv[...] = jnp.zeros(cv.shape, BF16)
        bk[...] = jnp.zeros(bk.shape, BF16)
        taps = f_ref[0, pl.ds(pl.multiple_of(step * per, per), per), :].astype(F32)
        for s in range(8):
            rolled[pl.ds(s, per, stride=8), :] = pltpu.roll(taps, s, 1) if s else taps
        docs = [docs_ref[b:b + 1, :] for b in range(blocks)]
        upper = lane >= row

        def more(p, carry):
            extras = extra_masks(docs, first, before, blocks, p * EXTRA)
            for g in range(per):
                here = pl.ds(CH * g, CH)
                low, _ = band_of(rolled[pl.ds(8 * g, 8), :], upper)
                p_here = jnp.concatenate([pt[x[0], here, :] * x[3] for x in extras], 0)
                z_here = jnp.concatenate([zt[x[0], here, :] * x[4] for x in extras], 0)
                conv = jnp.dot(p_here, low, preferred_element_type=F32).astype(BF16)
                back = lax.dot_general(z_here, low, (((1,), (1,)), ((), ())), preferred_element_type=F32).astype(BF16)
                for b in range(blocks):
                    acc, acb = cv[b, here, :], bk[b, here, :]
                    for e, x in enumerate(extras):
                        sl = slice(CH * e, CH * (e + 1))
                        acc = acc + conv[sl] * x[1][b]
                        acb = acb + back[sl] * x[2][b]
                    cv[b, here, :] = acc
                    bk[b, here, :] = acb
            return carry

        lax.fori_loop(1, (total + EXTRA - 1) // EXTRA, more, 0)
        for b in range(blocks):
            r = pl.ds(BLK * b, BLK)
            conv, back = cv[b].T.astype(F32), bk[b].T.astype(F32)
            go_ref[r, :] += (q_ref[r, :].astype(F32) * conv).astype(BF16)
            gq_ref[r, :] += (c_ref[r, :].astype(F32) * conv).astype(BF16)
            gk_ref[r, :] += (v_ref[r, :].astype(F32) * back).astype(BF16)
            gv_ref[r, :] += (k_ref[r, :].astype(F32) * back).astype(BF16)
        stores = [pltpu.make_async_copy(src, dst.at[:, cols], load_sem.at[i]) for i, (src, dst) in enumerate(
            ((go_ref, go_hbm), (gq_ref, gq_hbm), (gk_ref, gk_hbm), (gv_ref, gv_hbm)))]
        for copy in stores:
            copy.start()
        for copy in stores:
            copy.wait()
        return carry

    lax.fori_loop(0, jnp.where(total > EXTRA, tiles, 0), add_extras, 0)


def finish_call(grads, total, q, k, v, c, filters, docs):
    rows, chans = q.shape
    blocks, per = rows // BLK, TILE // CH
    anywhere, hbm = pl.BlockSpec(memory_space=pl.ANY), pl.BlockSpec(memory_space=pltpu.HBM)
    nat = jax.ShapeDtypeStruct((rows, chans), BF16)
    cell = pltpu.VMEM((rows, TILE), BF16)
    turned = pltpu.VMEM((blocks, TILE, BLK), BF16)
    return pl.pallas_call(
        functools.partial(finish_kernel, blocks, chans // TILE),
        out_shape=(nat, nat, nat, nat, jax.ShapeDtypeStruct(total.shape, F32)),
        in_specs=[anywhere] * 7 + [hbm] * 4,
        out_specs=(hbm,) * 5,
        scratch_shapes=[pltpu.SMEM(docs.shape, jnp.int32), pltpu.VMEM(docs.shape, jnp.int32), pltpu.VMEM(filters.shape, BF16),
                        pltpu.VMEM(total.shape, F32), pltpu.VMEM(total.shape, F32), pltpu.SemaphoreType.DMA((5,))] + [cell] * 8 + [turned] * 4 + [pltpu.VMEM((8 * per, BLK), F32),
                                                    pltpu.SemaphoreType.DMA((4, 2)), pltpu.SemaphoreType.DMA((8,))],
        compiler_params=pltpu.CompilerParams(vmem_limit_bytes=FINISH_VMEM),
        name="finish",
    )(docs, filters, total, *grads, q, k, v, c)


def local(queries, key_inputs, value_inputs, filters, doc_ids, cotangent):
    rows, chans = queries.shape
    groups, taps = filters.shape
    count, wide = lax.axis_size("seq"), lax.axis_size("tp")
    docs = doc_ids.reshape(rows // BLK, BLK)
    bank = filters.reshape(1, groups, taps)
    bound = 1.5 * math.sqrt(groups * wide * taps * (chans // groups) * rows * count)
    *grads, total = fused_call(count, wide, bound, queries, key_inputs, value_inputs, cotangent, bank, docs)
    return finish_call(grads, total, queries, key_inputs, value_inputs, cotangent, bank, docs)


def solution(mesh):
    cells, bank = P("seq", "tp"), P("tp", None)
    return jax.shard_map(local, mesh=mesh, in_specs=(cells, cells, cells, bank, P("seq"), cells),
                         out_specs=(cells, cells, cells, cells, bank), check_vma=False)
```

```python
import functools, math
import jax, jax.numpy as jnp
from jax import lax
from jax.experimental import pallas as pl
from jax.experimental.pallas import tpu as pltpu
from jax.sharding import PartitionSpec as P

BLK = 128
CH = 16
EXTRA = 4
QUAD = 4
TILE = 256
FUSED_VMEM = 49 * 2**20
FINISH_VMEM = 49 * 2**20
F32, BF16 = jnp.float32, jnp.bfloat16
MESH = pl.DeviceIdType.MESH


def block_docs(ids_ref, blocks):
    first = [ids_ref[b, 0] for b in range(blocks)]
    last = [ids_ref[b, BLK - 1] for b in range(blocks)]
    before = [jnp.int32(0)]
    for b in range(blocks):
        before.append(before[-1] + last[b] - first[b])
    return first, last, before


def extra_slot(first, before, blocks, e):
    b_of, doc = jnp.int32(0), first[0] + 1 + e
    for b in range(1, blocks):
        here = before[b] <= e
        b_of = jnp.where(here, b, b_of)
        doc = jnp.where(here, first[b] + 1 + e - before[b], doc)
    return b_of, doc


def mask_of(docs, doc, on=None):
    m = docs == doc
    if on is not None:
        m = m & on
    return jnp.broadcast_to(m.astype(F32), (CH, BLK)).astype(BF16)


def extra_masks(docs, first, before, blocks, start):
    total = before[blocks]
    out = []
    for e in range(EXTRA):
        b_e, doc_e = extra_slot(first, before, blocks, start + e)
        live = start + e < total
        xs = [mask_of(docs[b], doc_e, live & (b_e == b)) for b in range(blocks)]
        ys = [mask_of(docs[b], doc_e - 1, live & (b_e == b)) for b in range(blocks)]
        out.append((b_e, xs, ys, sum(xs[1:], xs[0]), sum(ys[1:], ys[0])))
    return out


def band_of(base, upper):
    ring = jnp.concatenate([pltpu.roll(base, 8 * r, 1) if r else base for r in range(BLK // 8)], axis=0)
    return jnp.where(upper, ring, 0.0).astype(BF16), jnp.where(upper, 0.0, ring).astype(BF16)


def wide_mul(a, b):
    return (a.astype(F32) * b.astype(F32)).astype(BF16)


def remote(src, dst, send_sem, recv_sem, to):
    return pltpu.make_async_remote_copy(src_ref=src, dst_ref=dst, send_sem=send_sem, recv_sem=recv_sem,
                                        device_id=to, device_id_type=MESH)


def start(copies):
    for copy in copies:
        copy.start()


def arrive(copies):
    for copy in copies:
        copy.wait_recv()


def fused_kernel(count, wide, bound, chans, rows_n,
                 docs_hbm, f_hbm, q_hbm, k_hbm, v_hbm, c_hbm,
                 go_hbm, gq_hbm, gk_hbm, gv_hbm, sum_ref,
                 ids_ref, docs_ref, f_ref, q_ref, k_ref, v_ref, c_ref, zn, pt, zt, cv, bk, o_go, o_gq, o_gk, o_gv,
                 c_rim, q_rim, p_out, p_in, z_out, z_in, ld_in, rd_in, rolled, folded, same, masks, part, got, ring, whole, energy,
                 known, small_sem, rim_sem, load_sem, save_sem, halo_s, halo_r,
                 send_a, recv_a, send_b, recv_b, send_c, recv_c, send_d, recv_d):
    me, tp = lax.axis_index("seq"), lax.axis_index("tp")
    blocks, groups, tiles = rows_n // BLK, chans // CH, chans // TILE
    per = TILE // CH
    tall = count // QUAD
    side, up = lax.rem(me, QUAD), me // QUAD
    slab = groups // QUAD
    right, left = lax.rem(me + 1, count), lax.rem(me + count - 1, count)

    def near(d):
        return {"seq": up * QUAD + lax.rem(side + d, QUAD), "tp": tp}

    def far(d):
        return {"seq": lax.rem(me + QUAD * d, count), "tp": tp}

    def plane(d, e):
        return {"seq": up * QUAD + lax.rem(side + d, QUAD), "tp": lax.rem(tp + e, wide)}

    def slab_rows(i):
        return pl.ds(pl.multiple_of(i * slab, slab), slab)

    barrier = pltpu.get_barrier_semaphore()
    line = wide // 2
    along = (tp // line) * line
    others = [{"seq": left, "tp": tp}, {"seq": right, "tp": tp}]
    others += [near(d) for d in range(1, QUAD)]
    others += [far(1), far(tall - 1)]
    others += [{"seq": me, "tp": along + lax.rem(tp + d, line)} for d in (1, line - 1)]
    others += [{"seq": me, "tp": lax.rem(tp + line, wide)}]

    def greet(sem):
        for to in others:
            pl.semaphore_signal(sem, inc=1, device_id=to, device_id_type=MESH)

    greet(barrier)

    small = [pltpu.make_async_copy(src, dst, small_sem.at[i]) for i, (src, dst) in enumerate(
        ((docs_hbm, ids_ref), (docs_hbm, docs_ref), (f_hbm, f_ref)))]
    tail, head = pl.ds(rows_n - BLK, BLK), pl.ds(0, BLK)
    rims = [pltpu.make_async_copy(src.at[head], dst, rim_sem.at[i]) for i, (src, dst) in enumerate(((c_hbm, c_rim), (q_hbm, q_rim)))]
    start(rims)
    start(small)
    loads = [[pltpu.make_async_copy(src.at[:, pl.ds(t * TILE, TILE)], dst.at[:, pl.ds(t * TILE, TILE)], load_sem.at[t, i])
              for i, (src, dst) in enumerate(((k_hbm, k_ref), (v_hbm, v_ref), (c_hbm, c_ref), (q_hbm, q_ref)))] for t in range(tiles)]
    for t in range(tiles):
        start(loads[t])

    def tile_cols(t):
        return pl.ds(t * TILE, TILE)

    to_left, to_right = {"seq": left, "tp": tp}, {"seq": right, "tp": tp}
    halo_z = [remote(z_out.at[:, tile_cols(t)], z_in.at[:, tile_cols(t)], halo_s.at[t], halo_r.at[t], to_left) for t in range(tiles)]
    halo_d = remote(docs_ref.at[pl.ds(0, 1)], rd_in, halo_s.at[tiles], halo_r.at[tiles], to_left)
    halo_p = [remote(p_out, p_in, halo_s.at[tiles + 1], halo_r.at[tiles + 1], to_right),
              remote(docs_ref.at[pl.ds(blocks - 1, 1)], ld_in, halo_s.at[tiles + 2], halo_r.at[tiles + 2], to_right)]
    scatter = [remote(part.at[slab_rows(lax.rem(side + d, QUAD))], got.at[d], send_a.at[d], recv_a.at[d], near(d))
               for d in range(1, QUAD)]
    climb = [remote(ring.at[up], ring.at[up], send_b.at[d], recv_b.at[d], far(d)) for d in range(1, tall)]
    spread = [remote(whole.at[slab_rows(side)], whole.at[slab_rows(side)], send_c.at[d], recv_c.at[d], near(d))
              for d in range(1, QUAD)]
    slot = side * wide + tp
    tell = [remote(energy.at[slot], energy.at[slot], send_d.at[d * wide + e], recv_d.at[d * wide + e], plane(d, e))
            for e in sorted(range(wide), key=lambda e: -min(e % (wide // 2), wide // 2 - e % (wide // 2))) for d in (2, 1, 3, 0) if d or e]

    row = lax.broadcasted_iota(jnp.int32, (BLK, BLK), 0)
    lane = lax.broadcasted_iota(jnp.int32, (BLK, BLK), 1)
    upper = lane >= row
    for copy in small:
        copy.wait()
    first, last, before = block_docs(ids_ref, blocks)
    docs = [docs_ref[b:b + 1, :] for b in range(blocks)]
    across = [jnp.broadcast_to(d.astype(F32), (BLK, BLK)) for d in docs]
    for b in range(blocks):
        same[b] = jnp.where((lane <= row) & (across[b].T == across[b]), 1.0, 0.0)
    m_cur = [mask_of(docs[b], first[b]) for b in range(blocks)]
    for b in range(blocks):
        masks[blocks + b] = m_cur[b]
    for b in range(1, blocks):
        masks[b] = mask_of(docs[b - 1], first[b])

    for copy in rims:
        copy.wait()
    z_out[...] = wide_mul(c_rim[...], q_rim[...])
    for t in range(tiles):
        for copy in loads[t]:
            copy.wait()
        cols = pl.ds(t * TILE, TILE)
        for b in range(blocks):
            r = pl.ds(BLK * b, BLK)
            pt[b + 1, cols, :] = wide_mul(k_ref[r, cols], v_ref[r, cols]).T
            z = wide_mul(c_ref[r, cols], q_ref[r, cols])
            zn[r, cols] = z
            zt[b, cols, :] = z.T
    pl.semaphore_wait(barrier, len(others))
    halo_d.start()
    start(halo_z)
    greet(known.at[0])

    nothing = jnp.zeros((CH, BLK), BF16)
    zero = jnp.concatenate([nothing, nothing], 1)
    octet = BLK // CH

    def beside(a, b):
        return [jnp.concatenate([a, nothing], 1), jnp.concatenate([nothing, b], 1)]

    def fold(acc):
        out = acc[:8]
        for r in range(1, BLK // 8):
            out = out + pltpu.roll(acc[8 * r:8 * r + 8], BLK - 8 * r, 1)
        return out

    def spot(t, g):
        return pl.multiple_of(t * TILE + CH * g, CH), pl.multiple_of(t * (TILE // 2) + 8 * g, 8)

    def inner_pairs(t, carry):
        for g in range(0, per, 2):
            h, k = g // octet, g % octet
            cols = pl.ds(pl.multiple_of(t * TILE + BLK * h, BLK), BLK)
            here = [pl.ds(spot(t, g + i)[0], CH) for i in range(2)]
            left_z, left_p = [], []
            for i in range(2):
                for b in range(1, blocks):
                    left_z.append(zt[b, here[i], :] * masks[blocks + b])
                    p = pt[b, here[i], :] * masks[b]
                    left_p.append(jnp.concatenate([nothing, p] if i else [p, nothing], 1))
                left_z.append(nothing)
                left_p.append(zero)
            prev = jnp.dot(jnp.concatenate(left_z, 0).T, jnp.concatenate(left_p, 0), preferred_element_type=F32)
            acc = [jnp.where(lane > row, prev[:, BLK * i:BLK * i + BLK], 0.0) for i in range(2)]
            for b in range(blocks):
                pad = jnp.concatenate([zero] * k + beside(pt[b + 1, here[0], :], pt[b + 1, here[1], :])
                                      + [zero] * (octet - 2 - k), 0)
                pair = jnp.dot(zn[pl.ds(BLK * b, BLK), cols], pad, preferred_element_type=F32)
                acc = [acc[i] + pair[:, BLK * i:BLK * i + BLK] * same[b] for i in range(2)]
            for i in range(2):
                folded[pl.ds(spot(t, g + i)[1], 8), :] = fold(acc[i])
        return carry

    lax.fori_loop(0, tiles // 2, inner_pairs, 0)
    p_out[...] = wide_mul(k_ref[tail, :], v_ref[tail, :])
    pl.semaphore_wait(known.at[0], len(others))
    greet(known.at[1])
    lax.fori_loop(tiles // 2, tiles, inner_pairs, 0)
    pl.semaphore_wait(known.at[1], len(others))
    greet(known.at[2])

    halo_d.wait_recv()
    rdocs = jnp.where(me == count - 1, -1, rd_in[...])
    beyond = jnp.broadcast_to(rdocs.astype(F32), (BLK, BLK)).T
    same[0] = jnp.where((lane > row) & (beyond == across[blocks - 1]), 1.0, 0.0)
    for t in range(tiles):
        halo_z[t].wait_recv()
        for g in range(0, per, 2):
            h, k = g // octet, g % octet
            cols = pl.ds(t * TILE + BLK * h, BLK)
            here = [pl.ds(t * TILE + CH * (g + i), CH) for i in range(2)]
            pad = jnp.concatenate([zero] * k + beside(pt[blocks, here[0], :], pt[blocks, here[1], :])
                                  + [zero] * (octet - 2 - k), 0)
            pair = jnp.dot(z_in[:, cols], pad, preferred_element_type=F32)
            for i in range(2):
                at = pl.ds(t * (TILE // 2) + 8 * (g + i), 8)
                folded[at, :] = folded[at, :] + fold(pair[:, BLK * i:BLK * i + BLK] * same[0])
    raw = folded[pl.ds(0, groups, stride=8), :]
    for i in range(1, 8):
        raw = raw + pltpu.roll(folded[pl.ds(i, groups, stride=8), :], BLK - i, 1)
    part[...] = raw
    start(scatter)
    start(halo_p)
    taps = f_ref[0].astype(F32)
    for s in range(8):
        rolled[pl.ds(s, groups, stride=8), :] = pltpu.roll(taps, s, 1) if s else taps

    d_next = docs[1:] + [rdocs]
    m_last = [mask_of(docs[b], last[b]) for b in range(blocks)]
    m_next = [mask_of(d_next[b], last[b]) for b in range(blocks)]
    extras = extra_masks(docs, first, before, blocks, 0)
    flat = m_last + m_next
    for _, xs, ys, x, y in extras:
        flat += xs + ys + [x, y]
    for i, m in enumerate(flat):
        masks[2 * blocks + i] = m

    def gates(t):
        def load(i):
            return masks[i]
        m_prev, m_cur, m_last, m_next = [[load(k * blocks + b) for b in range(blocks)] for k in range(4)]
        base_i, size = 4 * blocks, 2 * blocks + 2
        c2 = pl.ds(pl.multiple_of(t * TILE, TILE), TILE)
        pt[0, c2, :] = p_in[:, c2].T
        zt[blocks, c2, :] = z_in[:, c2].T
        cols = pl.ds(t * TILE, TILE) if isinstance(t, int) else pl.ds(pl.multiple_of(t * TILE, TILE), TILE)
        for g in range(per):
            here = pl.ds(t * TILE + CH * g, CH) if isinstance(t, int) else pl.ds(pl.multiple_of(t * TILE + CH * g, CH), CH)
            at8 = pl.ds(t * (TILE // 2) + 8 * g, 8) if isinstance(t, int) else pl.ds(pl.multiple_of(t * (TILE // 2) + 8 * g, 8), 8)
            local = pl.ds(CH * g, CH)
            low, high = band_of(rolled[at8, :], upper)
            p = [pt[b, here, :] for b in range(blocks + 1)]
            z = [zt[b, here, :] for b in range(blocks + 1)]
            p_left = [p[b] * m_prev[b] for b in range(blocks)]
            p_here = [p[b + 1] * m_cur[b] for b in range(blocks)]
            z_here = [z[b] * m_last[b] for b in range(blocks)]
            z_right = [z[b + 1] * m_next[b] for b in range(blocks)]
            for e in range(EXTRA):
                b_e = extras[e][0]
                p_left.append(nothing)
                p_here.append(pt[b_e + 1, here, :] * load(base_i + e * size + 2 * blocks))
                z_here.append(zt[b_e, here, :] * load(base_i + e * size + 2 * blocks + 1))
                z_right.append(nothing)
            p_win = jnp.concatenate([jnp.concatenate(p_left, 0), jnp.concatenate(p_here, 0)], 1)
            z_win = jnp.concatenate([jnp.concatenate(z_here, 0), jnp.concatenate(z_right, 0)], 1)
            conv = jnp.dot(p_win, jnp.concatenate([high, low], 0), preferred_element_type=F32).astype(BF16)
            back = lax.dot_general(z_win, jnp.concatenate([low, high], 1), (((1,), (1,)), ((), ())),
                                   preferred_element_type=F32).astype(BF16)
            for b in range(blocks):
                acc = conv[CH * b:CH * b + CH] * m_cur[b]
                acb = back[CH * b:CH * b + CH] * m_last[b]
                for e in range(EXTRA):
                    sl = slice(CH * (blocks + e), CH * (blocks + e + 1))
                    acc = acc + conv[sl] * load(base_i + e * size + b)
                    acb = acb + back[sl] * load(base_i + e * size + blocks + b)
                cv[b, local, :] = acc
                bk[b, local, :] = acb
        for b in range(blocks):
            r = pl.ds(BLK * b, BLK)
            conv, back = cv[b].T.astype(F32), bk[b].T.astype(F32)
            o_go[r, cols] = (q_ref[r, cols].astype(F32) * conv).astype(BF16)
            o_gq[r, cols] = (c_ref[r, cols].astype(F32) * conv).astype(BF16)
            o_gk[r, cols] = (v_ref[r, cols].astype(F32) * back).astype(BF16)
            o_gv[r, cols] = (k_ref[r, cols].astype(F32) * back).astype(BF16)

    def saves(t):
        cols = pl.ds(t * TILE, TILE)
        return [pltpu.make_async_copy(src.at[:, cols], dst.at[:, cols], save_sem.at[t, i]) for i, (src, dst) in enumerate(
            ((o_go, go_hbm), (o_gq, gq_hbm), (o_gk, gk_hbm), (o_gv, gv_hbm)))]

    cut = tiles // 2

    def run(a, b):
        lax.fori_loop(a, b, lambda t, carry: (gates(t), carry)[1], 0)
        for t in range(a, b):
            start(saves(t))

    arrive(scatter)
    mine = part[slab_rows(side), :]
    for d in range(1, QUAD):
        mine = mine + got[d]
    ring[up] = mine
    pl.semaphore_wait(known.at[2], len(others))
    start(climb)
    arrive(halo_p)
    masks[0] = mask_of(jnp.where(me == 0, -1, ld_in[...]), first[0])
    run(0, cut)
    arrive(climb)
    mine = ring[0]
    for z in range(1, tall):
        mine = mine + ring[z]
    whole[slab_rows(side), :] = mine
    energy[slot] = jnp.sum(mine * mine, axis=0, keepdims=True)
    start(spread)
    start(tell)
    run(cut, tiles)
    for t in range(tiles):
        for copy in saves(t):
            copy.wait()
    for copy in halo_z + [halo_d] + halo_p + scatter + climb:
        copy.wait_send()
    arrive(tell)
    arrive(spread)
    norm = jnp.sqrt(jnp.full((1, BLK), jnp.sum(energy[...]), F32))
    sum_ref[...] = whole[...] * jnp.minimum(1.0, bound / (norm + 1e-06))
    for copy in tell + spread:
        copy.wait_send()


def fused_call(count, wide, bound, q, k, v, c, filters, docs):
    rows, chans = q.shape
    blocks, groups, tiles = rows // BLK, chans // CH, chans // TILE
    tall = count // QUAD
    vm, anywhere = pl.BlockSpec(memory_space=pltpu.VMEM), pl.BlockSpec(memory_space=pl.ANY)
    hbm = pl.BlockSpec(memory_space=pltpu.HBM)
    nat = jax.ShapeDtypeStruct((rows, chans), BF16)
    dma = lambda *n: pltpu.SemaphoreType.DMA(n)
    big = pltpu.VMEM((rows, chans), BF16)
    rim = pltpu.VMEM((BLK, chans), BF16)
    line = pltpu.VMEM((1, BLK), jnp.int32)
    n_masks = 4 * blocks + EXTRA * (2 * blocks + 2)
    slab = groups // QUAD
    return pl.pallas_call(
        functools.partial(fused_kernel, count, wide, bound, chans, rows),
        out_shape=(nat, nat, nat, nat, jax.ShapeDtypeStruct((groups, BLK), F32)),
        in_specs=[anywhere] * 2 + [hbm] * 4,
        out_specs=(anywhere,) * 4 + (vm,),
        scratch_shapes=[pltpu.SMEM(docs.shape, jnp.int32), pltpu.VMEM(docs.shape, jnp.int32), pltpu.VMEM(filters.shape, BF16)]
        + [big] * 5 + [pltpu.VMEM((blocks + 1, chans, BLK), BF16)] * 2 + [pltpu.VMEM((blocks, TILE, BLK), BF16)] * 2
        + [big] * 4 + [rim] * 6 + [line] * 2
        + [pltpu.VMEM((8 * groups, BLK), F32)] * 2 + [pltpu.VMEM((blocks, BLK, BLK), F32), pltpu.VMEM((n_masks, CH, BLK), BF16),
           pltpu.VMEM((groups, BLK), F32), pltpu.VMEM((QUAD, slab, BLK), F32), pltpu.VMEM((tall, slab, BLK), F32),
           pltpu.VMEM((groups, BLK), F32), pltpu.VMEM((QUAD * wide, 1, BLK), F32)]
        + [pltpu.SemaphoreType.REGULAR((3,)), dma(3), dma(2), dma(tiles, 4), dma(tiles, 4), dma(tiles + 3), dma(tiles + 3),
           dma(QUAD), dma(QUAD), dma(tall), dma(tall), dma(QUAD), dma(QUAD), dma(QUAD * wide), dma(QUAD * wide)],
        compiler_params=pltpu.CompilerParams(collective_id=0, has_side_effects=True, vmem_limit_bytes=FUSED_VMEM),
        cost_estimate=pl.CostEstimate(flops=2 * 10**9, bytes_accessed=8 * 2**20, transcendentals=0),
        name="fused",
    )(docs, filters, q, k, v, c)


def finish_kernel(blocks, tiles, docs_hbm, f_hbm, total_hbm, a_go, a_gq, a_gk, a_gv, q_hbm, k_hbm, v_hbm, c_hbm,
                  go_hbm, gq_hbm, gk_hbm, gv_hbm, sum_hbm,
                  ids_ref, docs_ref, f_ref, total_ref, sum_ref, small_sem, q_ref, k_ref, v_ref, c_ref, go_ref, gq_ref, gk_ref, gv_ref, pt, zt, cv, bk, rolled, copy_sem, load_sem):
    per = TILE // CH
    rows = a_go.shape[0]
    half = rows // 2
    results = ((a_go, go_hbm), (a_gq, gq_hbm), (a_gk, gk_hbm), (a_gv, gv_hbm))
    copies = [pltpu.make_async_copy(src.at[pl.ds(h * half, half)], dst.at[pl.ds(h * half, half)], copy_sem.at[i, h])
              for i, (src, dst) in enumerate(results) for h in range(2)]
    for copy in copies:
        copy.start()
    small = [pltpu.make_async_copy(src, dst, small_sem.at[i]) for i, (src, dst) in enumerate(
        ((total_hbm, total_ref), (docs_hbm, ids_ref), (docs_hbm, docs_ref), (f_hbm, f_ref)))]
    start(small)
    row = lax.broadcasted_iota(jnp.int32, (BLK, BLK), 0)
    lane = lax.broadcasted_iota(jnp.int32, (BLK, BLK), 1)
    flip = (lane == (BLK - row) % BLK).astype(F32)
    small[0].wait()
    sum_ref[...] = jnp.dot(total_ref[...], flip, precision=lax.Precision.HIGHEST, preferred_element_type=F32)
    save = pltpu.make_async_copy(sum_ref, sum_hbm, small_sem.at[4])
    save.start()
    for copy in small[1:]:
        copy.wait()
    first, last, before = block_docs(ids_ref, blocks)
    total = before[blocks]
    save.wait()
    for copy in copies:
        copy.wait()

    def add_extras(step, carry):
        cols = pl.ds(pl.multiple_of(step * TILE, TILE), TILE)
        loads = [pltpu.make_async_copy(src.at[:, cols], dst, load_sem.at[i]) for i, (src, dst) in enumerate(
            ((q_hbm, q_ref), (k_hbm, k_ref), (v_hbm, v_ref), (c_hbm, c_ref),
             (a_go, go_ref), (a_gq, gq_ref), (a_gk, gk_ref), (a_gv, gv_ref)))]
        for copy in loads:
            copy.start()
        for copy in loads:
            copy.wait()
        for b in range(blocks):
            r = pl.ds(BLK * b, BLK)
            pt[b] = wide_mul(k_ref[r, :], v_ref[r, :]).T
            zt[b] = wide_mul(c_ref[r, :], q_ref[r, :]).T
        cv[...] = jnp.zeros(cv.shape, BF16)
        bk[...] = jnp.zeros(bk.shape, BF16)
        taps = f_ref[0, pl.ds(pl.multiple_of(step * per, per), per), :].astype(F32)
        for s in range(8):
            rolled[pl.ds(s, per, stride=8), :] = pltpu.roll(taps, s, 1) if s else taps
        docs = [docs_ref[b:b + 1, :] for b in range(blocks)]
        upper = lane >= row

        def more(p, carry):
            extras = extra_masks(docs, first, before, blocks, p * EXTRA)
            for g in range(per):
                here = pl.ds(CH * g, CH)
                low, _ = band_of(rolled[pl.ds(8 * g, 8), :], upper)
                p_here = jnp.concatenate([pt[x[0], here, :] * x[3] for x in extras], 0)
                z_here = jnp.concatenate([zt[x[0], here, :] * x[4] for x in extras], 0)
                conv = jnp.dot(p_here, low, preferred_element_type=F32).astype(BF16)
                back = lax.dot_general(z_here, low, (((1,), (1,)), ((), ())), preferred_element_type=F32).astype(BF16)
                for b in range(blocks):
                    acc, acb = cv[b, here, :], bk[b, here, :]
                    for e, x in enumerate(extras):
                        sl = slice(CH * e, CH * (e + 1))
                        acc = acc + conv[sl] * x[1][b]
                        acb = acb + back[sl] * x[2][b]
                    cv[b, here, :] = acc
                    bk[b, here, :] = acb
            return carry

        lax.fori_loop(1, (total + EXTRA - 1) // EXTRA, more, 0)
        for b in range(blocks):
            r = pl.ds(BLK * b, BLK)
            conv, back = cv[b].T.astype(F32), bk[b].T.astype(F32)
            go_ref[r, :] += (q_ref[r, :].astype(F32) * conv).astype(BF16)
            gq_ref[r, :] += (c_ref[r, :].astype(F32) * conv).astype(BF16)
            gk_ref[r, :] += (v_ref[r, :].astype(F32) * back).astype(BF16)
            gv_ref[r, :] += (k_ref[r, :].astype(F32) * back).astype(BF16)
        stores = [pltpu.make_async_copy(src, dst.at[:, cols], load_sem.at[i]) for i, (src, dst) in enumerate(
            ((go_ref, go_hbm), (gq_ref, gq_hbm), (gk_ref, gk_hbm), (gv_ref, gv_hbm)))]
        for copy in stores:
            copy.start()
        for copy in stores:
            copy.wait()
        return carry

    lax.fori_loop(0, jnp.where(total > EXTRA, tiles, 0), add_extras, 0)


def finish_call(grads, total, q, k, v, c, filters, docs):
    rows, chans = q.shape
    blocks, per = rows // BLK, TILE // CH
    anywhere, hbm = pl.BlockSpec(memory_space=pl.ANY), pl.BlockSpec(memory_space=pltpu.HBM)
    nat = jax.ShapeDtypeStruct((rows, chans), BF16)
    cell = pltpu.VMEM((rows, TILE), BF16)
    turned = pltpu.VMEM((blocks, TILE, BLK), BF16)
    return pl.pallas_call(
        functools.partial(finish_kernel, blocks, chans // TILE),
        out_shape=(nat, nat, nat, nat, jax.ShapeDtypeStruct(total.shape, F32)),
        in_specs=[anywhere] * 7 + [hbm] * 4,
        out_specs=(hbm,) * 5,
        scratch_shapes=[pltpu.SMEM(docs.shape, jnp.int32), pltpu.VMEM(docs.shape, jnp.int32), pltpu.VMEM(filters.shape, BF16),
                        pltpu.VMEM(total.shape, F32), pltpu.VMEM(total.shape, F32), pltpu.SemaphoreType.DMA((5,))] + [cell] * 8 + [turned] * 4 + [pltpu.VMEM((8 * per, BLK), F32),
                                                    pltpu.SemaphoreType.DMA((4, 2)), pltpu.SemaphoreType.DMA((8,))],
        compiler_params=pltpu.CompilerParams(vmem_limit_bytes=FINISH_VMEM),
        name="finish",
    )(docs, filters, total, *grads, q, k, v, c)


def local(queries, key_inputs, value_inputs, filters, doc_ids, cotangent):
    rows, chans = queries.shape
    groups, taps = filters.shape
    count, wide = lax.axis_size("seq"), lax.axis_size("tp")
    docs = doc_ids.reshape(rows // BLK, BLK)
    bank = filters.reshape(1, groups, taps)
    bound = 1.5 * math.sqrt(groups * wide * taps * (chans // groups) * rows * count)
    *grads, total = fused_call(count, wide, bound, queries, key_inputs, value_inputs, cotangent, bank, docs)
    return finish_call(grads, total, queries, key_inputs, value_inputs, cotangent, bank, docs)


def solution(mesh):
    cells, bank = P("seq", "tp"), P("tp", None)
    return jax.shard_map(local, mesh=mesh, in_specs=(cells, cells, cells, bank, P("seq"), cells),
                         out_specs=(cells, cells, cells, cells, bank), check_vma=False)
```

```python
import functools, math
import jax, jax.numpy as jnp
from jax import lax
from jax.experimental import pallas as pl
from jax.experimental.pallas import tpu as pltpu
from jax.sharding import PartitionSpec as P

BLK = 128
CH = 16
EXTRA = 4
QUAD = 4
TILE = 256
FUSED_VMEM = 49 * 2**20
FINISH_VMEM = 49 * 2**20
F32, BF16 = jnp.float32, jnp.bfloat16
MESH = pl.DeviceIdType.MESH


def block_docs(ids_ref, blocks):
    first = [ids_ref[b, 0] for b in range(blocks)]
    last = [ids_ref[b, BLK - 1] for b in range(blocks)]
    before = [jnp.int32(0)]
    for b in range(blocks):
        before.append(before[-1] + last[b] - first[b])
    return first, last, before


def extra_slot(first, before, blocks, e):
    b_of, doc = jnp.int32(0), first[0] + 1 + e
    for b in range(1, blocks):
        here = before[b] <= e
        b_of = jnp.where(here, b, b_of)
        doc = jnp.where(here, first[b] + 1 + e - before[b], doc)
    return b_of, doc


def mask_of(docs, doc, on=None):
    m = docs == doc
    if on is not None:
        m = m & on
    return jnp.broadcast_to(m.astype(F32), (CH, BLK)).astype(BF16)


def extra_masks(docs, first, before, blocks, start):
    total = before[blocks]
    out = []
    for e in range(EXTRA):
        b_e, doc_e = extra_slot(first, before, blocks, start + e)
        live = start + e < total
        xs = [mask_of(docs[b], doc_e, live & (b_e == b)) for b in range(blocks)]
        ys = [mask_of(docs[b], doc_e - 1, live & (b_e == b)) for b in range(blocks)]
        out.append((b_e, xs, ys, sum(xs[1:], xs[0]), sum(ys[1:], ys[0])))
    return out


def band_of(base, upper):
    ring = jnp.concatenate([pltpu.roll(base, 8 * r, 1) if r else base for r in range(BLK // 8)], axis=0)
    return jnp.where(upper, ring, 0.0).astype(BF16), jnp.where(upper, 0.0, ring).astype(BF16)


def wide_mul(a, b):
    return (a.astype(F32) * b.astype(F32)).astype(BF16)


def remote(src, dst, send_sem, recv_sem, to):
    return pltpu.make_async_remote_copy(src_ref=src, dst_ref=dst, send_sem=send_sem, recv_sem=recv_sem,
                                        device_id=to, device_id_type=MESH)


def start(copies):
    for copy in copies:
        copy.start()


def arrive(copies):
    for copy in copies:
        copy.wait_recv()


def fused_kernel(count, wide, bound, chans, rows_n,
                 docs_hbm, f_hbm, q_hbm, k_hbm, v_hbm, c_hbm,
                 go_hbm, gq_hbm, gk_hbm, gv_hbm, sum_ref,
                 ids_ref, docs_ref, f_ref, q_ref, k_ref, v_ref, c_ref, zn, pt, zt, cv, bk, o_go, o_gq, o_gk, o_gv,
                 c_rim, q_rim, p_out, p_in, z_out, z_in, ld_in, rd_in, rolled, folded, same, masks, part, got, ring, whole, energy,
                 known, small_sem, rim_sem, load_sem, save_sem, halo_s, halo_r,
                 send_a, recv_a, send_b, recv_b, send_c, recv_c, send_d, recv_d):
    me, tp = lax.axis_index("seq"), lax.axis_index("tp")
    blocks, groups, tiles = rows_n // BLK, chans // CH, chans // TILE
    per = TILE // CH
    tall = count // QUAD
    side, up = lax.rem(me, QUAD), me // QUAD
    slab = groups // QUAD
    right, left = lax.rem(me + 1, count), lax.rem(me + count - 1, count)

    def near(d):
        return {"seq": up * QUAD + lax.rem(side + d, QUAD), "tp": tp}

    def far(d):
        return {"seq": lax.rem(me + QUAD * d, count), "tp": tp}

    def plane(d, e):
        return {"seq": up * QUAD + lax.rem(side + d, QUAD), "tp": lax.rem(tp + e, wide)}

    def slab_rows(i):
        return pl.ds(pl.multiple_of(i * slab, slab), slab)

    barrier = pltpu.get_barrier_semaphore()
    line = wide // 2
    along = (tp // line) * line
    others = [{"seq": left, "tp": tp}, {"seq": right, "tp": tp}]
    others += [near(d) for d in range(1, QUAD)]
    others += [far(1), far(tall - 1)]
    others += [{"seq": me, "tp": along + lax.rem(tp + d, line)} for d in (1, line - 1)]
    others += [{"seq": me, "tp": lax.rem(tp + line, wide)}]

    def greet(sem):
        for to in others:
            pl.semaphore_signal(sem, inc=1, device_id=to, device_id_type=MESH)

    greet(barrier)

    small = [pltpu.make_async_copy(src, dst, small_sem.at[i]) for i, (src, dst) in enumerate(
        ((docs_hbm, ids_ref), (docs_hbm, docs_ref), (f_hbm, f_ref)))]
    tail, head = pl.ds(rows_n - BLK, BLK), pl.ds(0, BLK)
    rims = [pltpu.make_async_copy(src.at[head], dst, rim_sem.at[i]) for i, (src, dst) in enumerate(((c_hbm, c_rim), (q_hbm, q_rim)))]
    start(rims)
    start(small)
    loads = [[pltpu.make_async_copy(src.at[:, pl.ds(t * TILE, TILE)], dst.at[:, pl.ds(t * TILE, TILE)], load_sem.at[t, i])
              for i, (src, dst) in enumerate(((k_hbm, k_ref), (v_hbm, v_ref), (c_hbm, c_ref), (q_hbm, q_ref)))] for t in range(tiles)]
    for t in range(tiles):
        start(loads[t])

    def tile_cols(t):
        return pl.ds(t * TILE, TILE)

    to_left, to_right = {"seq": left, "tp": tp}, {"seq": right, "tp": tp}
    halo_z = [remote(z_out.at[:, tile_cols(t)], z_in.at[:, tile_cols(t)], halo_s.at[t], halo_r.at[t], to_left) for t in range(tiles)]
    halo_d = remote(docs_ref.at[pl.ds(0, 1)], rd_in, halo_s.at[tiles], halo_r.at[tiles], to_left)
    halo_p = [remote(p_out, p_in, halo_s.at[tiles + 1], halo_r.at[tiles + 1], to_right),
              remote(docs_ref.at[pl.ds(blocks - 1, 1)], ld_in, halo_s.at[tiles + 2], halo_r.at[tiles + 2], to_right)]
    scatter = [remote(part.at[slab_rows(lax.rem(side + d, QUAD))], got.at[d], send_a.at[d], recv_a.at[d], near(d))
               for d in range(1, QUAD)]
    climb = [remote(ring.at[up], ring.at[up], send_b.at[d], recv_b.at[d], far(d)) for d in range(1, tall)]
    spread = [remote(whole.at[slab_rows(side)], whole.at[slab_rows(side)], send_c.at[d], recv_c.at[d], near(d))
              for d in range(1, QUAD)]
    slot = side * wide + tp
    tell = [remote(energy.at[slot], energy.at[slot], send_d.at[d * wide + e], recv_d.at[d * wide + e], plane(d, e))
            for e in sorted(range(wide), key=lambda e: -min(e % (wide // 2), wide // 2 - e % (wide // 2))) for d in (2, 1, 3, 0) if d or e]

    row = lax.broadcasted_iota(jnp.int32, (BLK, BLK), 0)
    lane = lax.broadcasted_iota(jnp.int32, (BLK, BLK), 1)
    upper = lane >= row
    for copy in small:
        copy.wait()
    first, last, before = block_docs(ids_ref, blocks)
    docs = [docs_ref[b:b + 1, :] for b in range(blocks)]
    across = [jnp.broadcast_to(d.astype(F32), (BLK, BLK)) for d in docs]
    for b in range(blocks):
        same[b] = jnp.where((lane <= row) & (across[b].T == across[b]), 1.0, 0.0)
    m_cur = [mask_of(docs[b], first[b]) for b in range(blocks)]
    for b in range(blocks):
        masks[blocks + b] = m_cur[b]
    for b in range(1, blocks):
        masks[b] = mask_of(docs[b - 1], first[b])

    for copy in rims:
        copy.wait()
    z_out[...] = wide_mul(c_rim[...], q_rim[...])
    pl.semaphore_wait(barrier, len(others))
    halo_d.start()
    start(halo_z)
    greet(known.at[0])
    for t in range(tiles):
        for copy in loads[t]:
            copy.wait()
        cols = pl.ds(t * TILE, TILE)
        for b in range(blocks):
            r = pl.ds(BLK * b, BLK)
            pt[b + 1, cols, :] = wide_mul(k_ref[r, cols], v_ref[r, cols]).T
            z = wide_mul(c_ref[r, cols], q_ref[r, cols])
            zn[r, cols] = z
            zt[b, cols, :] = z.T

    nothing = jnp.zeros((CH, BLK), BF16)
    zero = jnp.concatenate([nothing, nothing], 1)
    octet = BLK // CH

    def beside(a, b):
        return [jnp.concatenate([a, nothing], 1), jnp.concatenate([nothing, b], 1)]

    def fold(acc):
        out = acc[:8]
        for r in range(1, BLK // 8):
            out = out + pltpu.roll(acc[8 * r:8 * r + 8], BLK - 8 * r, 1)
        return out

    def spot(t, g):
        return pl.multiple_of(t * TILE + CH * g, CH), pl.multiple_of(t * (TILE // 2) + 8 * g, 8)

    def inner_pairs(t, carry):
        for g in range(0, per, 2):
            h, k = g // octet, g % octet
            cols = pl.ds(pl.multiple_of(t * TILE + BLK * h, BLK), BLK)
            here = [pl.ds(spot(t, g + i)[0], CH) for i in range(2)]
            left_z, left_p = [], []
            for i in range(2):
                for b in range(1, blocks):
                    left_z.append(zt[b, here[i], :] * masks[blocks + b])
                    p = pt[b, here[i], :] * masks[b]
                    left_p.append(jnp.concatenate([nothing, p] if i else [p, nothing], 1))
                left_z.append(nothing)
                left_p.append(zero)
            prev = jnp.dot(jnp.concatenate(left_z, 0).T, jnp.concatenate(left_p, 0), preferred_element_type=F32)
            acc = [jnp.where(lane > row, prev[:, BLK * i:BLK * i + BLK], 0.0) for i in range(2)]
            for b in range(blocks):
                pad = jnp.concatenate([zero] * k + beside(pt[b + 1, here[0], :], pt[b + 1, here[1], :])
                                      + [zero] * (octet - 2 - k), 0)
                pair = jnp.dot(zn[pl.ds(BLK * b, BLK), cols], pad, preferred_element_type=F32)
                acc = [acc[i] + pair[:, BLK * i:BLK * i + BLK] * same[b] for i in range(2)]
            for i in range(2):
                folded[pl.ds(spot(t, g + i)[1], 8), :] = fold(acc[i])
        return carry

    lax.fori_loop(0, tiles // 2, inner_pairs, 0)
    p_out[...] = wide_mul(k_ref[tail, :], v_ref[tail, :])
    pl.semaphore_wait(known.at[0], len(others))
    greet(known.at[1])
    lax.fori_loop(tiles // 2, tiles, inner_pairs, 0)
    pl.semaphore_wait(known.at[1], len(others))
    greet(known.at[2])

    halo_d.wait_recv()
    rdocs = jnp.where(me == count - 1, -1, rd_in[...])
    beyond = jnp.broadcast_to(rdocs.astype(F32), (BLK, BLK)).T
    same[0] = jnp.where((lane > row) & (beyond == across[blocks - 1]), 1.0, 0.0)
    for t in range(tiles):
        halo_z[t].wait_recv()
        for g in range(0, per, 2):
            h, k = g // octet, g % octet
            cols = pl.ds(t * TILE + BLK * h, BLK)
            here = [pl.ds(t * TILE + CH * (g + i), CH) for i in range(2)]
            pad = jnp.concatenate([zero] * k + beside(pt[blocks, here[0], :], pt[blocks, here[1], :])
                                  + [zero] * (octet - 2 - k), 0)
            pair = jnp.dot(z_in[:, cols], pad, preferred_element_type=F32)
            for i in range(2):
                at = pl.ds(t * (TILE // 2) + 8 * (g + i), 8)
                folded[at, :] = folded[at, :] + fold(pair[:, BLK * i:BLK * i + BLK] * same[0])
    raw = folded[pl.ds(0, groups, stride=8), :]
    for i in range(1, 8):
        raw = raw + pltpu.roll(folded[pl.ds(i, groups, stride=8), :], BLK - i, 1)
    part[...] = raw
    start(scatter)
    start(halo_p)
    taps = f_ref[0].astype(F32)
    for s in range(8):
        rolled[pl.ds(s, groups, stride=8), :] = pltpu.roll(taps, s, 1) if s else taps

    d_next = docs[1:] + [rdocs]
    m_last = [mask_of(docs[b], last[b]) for b in range(blocks)]
    m_next = [mask_of(d_next[b], last[b]) for b in range(blocks)]
    extras = extra_masks(docs, first, before, blocks, 0)
    flat = m_last + m_next
    for _, xs, ys, x, y in extras:
        flat += xs + ys + [x, y]
    for i, m in enumerate(flat):
        masks[2 * blocks + i] = m

    def gates(t):
        def load(i):
            return masks[i]
        m_prev, m_cur, m_last, m_next = [[load(k * blocks + b) for b in range(blocks)] for k in range(4)]
        base_i, size = 4 * blocks, 2 * blocks + 2
        c2 = pl.ds(pl.multiple_of(t * TILE, TILE), TILE)
        pt[0, c2, :] = p_in[:, c2].T
        zt[blocks, c2, :] = z_in[:, c2].T
        cols = pl.ds(t * TILE, TILE) if isinstance(t, int) else pl.ds(pl.multiple_of(t * TILE, TILE), TILE)
        for g in range(per):
            here = pl.ds(t * TILE + CH * g, CH) if isinstance(t, int) else pl.ds(pl.multiple_of(t * TILE + CH * g, CH), CH)
            at8 = pl.ds(t * (TILE // 2) + 8 * g, 8) if isinstance(t, int) else pl.ds(pl.multiple_of(t * (TILE // 2) + 8 * g, 8), 8)
            local = pl.ds(CH * g, CH)
            low, high = band_of(rolled[at8, :], upper)
            p = [pt[b, here, :] for b in range(blocks + 1)]
            z = [zt[b, here, :] for b in range(blocks + 1)]
            p_left = [p[b] * m_prev[b] for b in range(blocks)]
            p_here = [p[b + 1] * m_cur[b] for b in range(blocks)]
            z_here = [z[b] * m_last[b] for b in range(blocks)]
            z_right = [z[b + 1] * m_next[b] for b in range(blocks)]
            for e in range(EXTRA):
                b_e = extras[e][0]
                p_left.append(nothing)
                p_here.append(pt[b_e + 1, here, :] * load(base_i + e * size + 2 * blocks))
                z_here.append(zt[b_e, here, :] * load(base_i + e * size + 2 * blocks + 1))
                z_right.append(nothing)
            p_win = jnp.concatenate([jnp.concatenate(p_left, 0), jnp.concatenate(p_here, 0)], 1)
            z_win = jnp.concatenate([jnp.concatenate(z_here, 0), jnp.concatenate(z_right, 0)], 1)
            conv = jnp.dot(p_win, jnp.concatenate([high, low], 0), preferred_element_type=F32).astype(BF16)
            back = lax.dot_general(z_win, jnp.concatenate([low, high], 1), (((1,), (1,)), ((), ())),
                                   preferred_element_type=F32).astype(BF16)
            for b in range(blocks):
                acc = conv[CH * b:CH * b + CH] * m_cur[b]
                acb = back[CH * b:CH * b + CH] * m_last[b]
                for e in range(EXTRA):
                    sl = slice(CH * (blocks + e), CH * (blocks + e + 1))
                    acc = acc + conv[sl] * load(base_i + e * size + b)
                    acb = acb + back[sl] * load(base_i + e * size + blocks + b)
                cv[b, local, :] = acc
                bk[b, local, :] = acb
        for b in range(blocks):
            r = pl.ds(BLK * b, BLK)
            conv, back = cv[b].T.astype(F32), bk[b].T.astype(F32)
            o_go[r, cols] = (q_ref[r, cols].astype(F32) * conv).astype(BF16)
            o_gq[r, cols] = (c_ref[r, cols].astype(F32) * conv).astype(BF16)
            o_gk[r, cols] = (v_ref[r, cols].astype(F32) * back).astype(BF16)
            o_gv[r, cols] = (k_ref[r, cols].astype(F32) * back).astype(BF16)

    def saves(t):
        cols = pl.ds(t * TILE, TILE)
        return [pltpu.make_async_copy(src.at[:, cols], dst.at[:, cols], save_sem.at[t, i]) for i, (src, dst) in enumerate(
            ((o_go, go_hbm), (o_gq, gq_hbm), (o_gk, gk_hbm), (o_gv, gv_hbm)))]

    cut = tiles // 2

    def run(a, b):
        lax.fori_loop(a, b, lambda t, carry: (gates(t), carry)[1], 0)
        for t in range(a, b):
            start(saves(t))

    arrive(scatter)
    mine = part[slab_rows(side), :]
    for d in range(1, QUAD):
        mine = mine + got[d]
    ring[up] = mine
    pl.semaphore_wait(known.at[2], len(others))
    start(climb)
    arrive(halo_p)
    masks[0] = mask_of(jnp.where(me == 0, -1, ld_in[...]), first[0])
    run(0, cut)
    arrive(climb)
    mine = ring[0]
    for z in range(1, tall):
        mine = mine + ring[z]
    whole[slab_rows(side), :] = mine
    energy[slot] = jnp.sum(mine * mine, axis=0, keepdims=True)
    start(spread)
    start(tell)
    run(cut, tiles)
    for t in range(tiles):
        for copy in saves(t):
            copy.wait()
    for copy in halo_z + [halo_d] + halo_p + scatter + climb:
        copy.wait_send()
    arrive(tell)
    arrive(spread)
    norm = jnp.sqrt(jnp.full((1, BLK), jnp.sum(energy[...]), F32))
    sum_ref[...] = whole[...] * jnp.minimum(1.0, bound / (norm + 1e-06))
    for copy in tell + spread:
        copy.wait_send()


def fused_call(count, wide, bound, q, k, v, c, filters, docs):
    rows, chans = q.shape
    blocks, groups, tiles = rows // BLK, chans // CH, chans // TILE
    tall = count // QUAD
    vm, anywhere = pl.BlockSpec(memory_space=pltpu.VMEM), pl.BlockSpec(memory_space=pl.ANY)
    hbm = pl.BlockSpec(memory_space=pltpu.HBM)
    nat = jax.ShapeDtypeStruct((rows, chans), BF16)
    dma = lambda *n: pltpu.SemaphoreType.DMA(n)
    big = pltpu.VMEM((rows, chans), BF16)
    rim = pltpu.VMEM((BLK, chans), BF16)
    line = pltpu.VMEM((1, BLK), jnp.int32)
    n_masks = 4 * blocks + EXTRA * (2 * blocks + 2)
    slab = groups // QUAD
    return pl.pallas_call(
        functools.partial(fused_kernel, count, wide, bound, chans, rows),
        out_shape=(nat, nat, nat, nat, jax.ShapeDtypeStruct((groups, BLK), F32)),
        in_specs=[anywhere] * 2 + [hbm] * 4,
        out_specs=(anywhere,) * 4 + (vm,),
        scratch_shapes=[pltpu.SMEM(docs.shape, jnp.int32), pltpu.VMEM(docs.shape, jnp.int32), pltpu.VMEM(filters.shape, BF16)]
        + [big] * 5 + [pltpu.VMEM((blocks + 1, chans, BLK), BF16)] * 2 + [pltpu.VMEM((blocks, TILE, BLK), BF16)] * 2
        + [big] * 4 + [rim] * 6 + [line] * 2
        + [pltpu.VMEM((8 * groups, BLK), F32)] * 2 + [pltpu.VMEM((blocks, BLK, BLK), F32), pltpu.VMEM((n_masks, CH, BLK), BF16),
           pltpu.VMEM((groups, BLK), F32), pltpu.VMEM((QUAD, slab, BLK), F32), pltpu.VMEM((tall, slab, BLK), F32),
           pltpu.VMEM((groups, BLK), F32), pltpu.VMEM((QUAD * wide, 1, BLK), F32)]
        + [pltpu.SemaphoreType.REGULAR((3,)), dma(3), dma(2), dma(tiles, 4), dma(tiles, 4), dma(tiles + 3), dma(tiles + 3),
           dma(QUAD), dma(QUAD), dma(tall), dma(tall), dma(QUAD), dma(QUAD), dma(QUAD * wide), dma(QUAD * wide)],
        compiler_params=pltpu.CompilerParams(collective_id=0, has_side_effects=True, vmem_limit_bytes=FUSED_VMEM),
        cost_estimate=pl.CostEstimate(flops=2 * 10**9, bytes_accessed=8 * 2**20, transcendentals=0),
        name="fused",
    )(docs, filters, q, k, v, c)


def finish_kernel(blocks, tiles, docs_hbm, f_hbm, total_hbm, a_go, a_gq, a_gk, a_gv, q_hbm, k_hbm, v_hbm, c_hbm,
                  go_hbm, gq_hbm, gk_hbm, gv_hbm, sum_hbm,
                  ids_ref, docs_ref, f_ref, total_ref, sum_ref, small_sem, q_ref, k_ref, v_ref, c_ref, go_ref, gq_ref, gk_ref, gv_ref, pt, zt, cv, bk, rolled, copy_sem, load_sem):
    per = TILE // CH
    rows = a_go.shape[0]
    half = rows // 2
    results = ((a_go, go_hbm), (a_gq, gq_hbm), (a_gk, gk_hbm), (a_gv, gv_hbm))
    copies = [pltpu.make_async_copy(src.at[pl.ds(h * half, half)], dst.at[pl.ds(h * half, half)], copy_sem.at[i, h])
              for i, (src, dst) in enumerate(results) for h in range(2)]
    for copy in copies:
        copy.start()
    small = [pltpu.make_async_copy(src, dst, small_sem.at[i]) for i, (src, dst) in enumerate(
        ((total_hbm, total_ref), (docs_hbm, ids_ref), (docs_hbm, docs_ref), (f_hbm, f_ref)))]
    start(small)
    row = lax.broadcasted_iota(jnp.int32, (BLK, BLK), 0)
    lane = lax.broadcasted_iota(jnp.int32, (BLK, BLK), 1)
    flip = (lane == (BLK - row) % BLK).astype(F32)
    small[0].wait()
    sum_ref[...] = jnp.dot(total_ref[...], flip, precision=lax.Precision.HIGHEST, preferred_element_type=F32)
    save = pltpu.make_async_copy(sum_ref, sum_hbm, small_sem.at[4])
    save.start()
    for copy in small[1:]:
        copy.wait()
    first, last, before = block_docs(ids_ref, blocks)
    total = before[blocks]
    save.wait()
    for copy in copies:
        copy.wait()

    def add_extras(step, carry):
        cols = pl.ds(pl.multiple_of(step * TILE, TILE), TILE)
        loads = [pltpu.make_async_copy(src.at[:, cols], dst, load_sem.at[i]) for i, (src, dst) in enumerate(
            ((q_hbm, q_ref), (k_hbm, k_ref), (v_hbm, v_ref), (c_hbm, c_ref),
             (a_go, go_ref), (a_gq, gq_ref), (a_gk, gk_ref), (a_gv, gv_ref)))]
        for copy in loads:
            copy.start()
        for copy in loads:
            copy.wait()
        for b in range(blocks):
            r = pl.ds(BLK * b, BLK)
            pt[b] = wide_mul(k_ref[r, :], v_ref[r, :]).T
            zt[b] = wide_mul(c_ref[r, :], q_ref[r, :]).T
        cv[...] = jnp.zeros(cv.shape, BF16)
        bk[...] = jnp.zeros(bk.shape, BF16)
        taps = f_ref[0, pl.ds(pl.multiple_of(step * per, per), per), :].astype(F32)
        for s in range(8):
            rolled[pl.ds(s, per, stride=8), :] = pltpu.roll(taps, s, 1) if s else taps
        docs = [docs_ref[b:b + 1, :] for b in range(blocks)]
        upper = lane >= row

        def more(p, carry):
            extras = extra_masks(docs, first, before, blocks, p * EXTRA)
            for g in range(per):
                here = pl.ds(CH * g, CH)
                low, _ = band_of(rolled[pl.ds(8 * g, 8), :], upper)
                p_here = jnp.concatenate([pt[x[0], here, :] * x[3] for x in extras], 0)
                z_here = jnp.concatenate([zt[x[0], here, :] * x[4] for x in extras], 0)
                conv = jnp.dot(p_here, low, preferred_element_type=F32).astype(BF16)
                back = lax.dot_general(z_here, low, (((1,), (1,)), ((), ())), preferred_element_type=F32).astype(BF16)
                for b in range(blocks):
                    acc, acb = cv[b, here, :], bk[b, here, :]
                    for e, x in enumerate(extras):
                        sl = slice(CH * e, CH * (e + 1))
                        acc = acc + conv[sl] * x[1][b]
                        acb = acb + back[sl] * x[2][b]
                    cv[b, here, :] = acc
                    bk[b, here, :] = acb
            return carry

        lax.fori_loop(1, (total + EXTRA - 1) // EXTRA, more, 0)
        for b in range(blocks):
            r = pl.ds(BLK * b, BLK)
            conv, back = cv[b].T.astype(F32), bk[b].T.astype(F32)
            go_ref[r, :] += (q_ref[r, :].astype(F32) * conv).astype(BF16)
            gq_ref[r, :] += (c_ref[r, :].astype(F32) * conv).astype(BF16)
            gk_ref[r, :] += (v_ref[r, :].astype(F32) * back).astype(BF16)
            gv_ref[r, :] += (k_ref[r, :].astype(F32) * back).astype(BF16)
        stores = [pltpu.make_async_copy(src, dst.at[:, cols], load_sem.at[i]) for i, (src, dst) in enumerate(
            ((go_ref, go_hbm), (gq_ref, gq_hbm), (gk_ref, gk_hbm), (gv_ref, gv_hbm)))]
        for copy in stores:
            copy.start()
        for copy in stores:
            copy.wait()
        return carry

    lax.fori_loop(0, jnp.where(total > EXTRA, tiles, 0), add_extras, 0)


def finish_call(grads, total, q, k, v, c, filters, docs):
    rows, chans = q.shape
    blocks, per = rows // BLK, TILE // CH
    anywhere, hbm = pl.BlockSpec(memory_space=pl.ANY), pl.BlockSpec(memory_space=pltpu.HBM)
    nat = jax.ShapeDtypeStruct((rows, chans), BF16)
    cell = pltpu.VMEM((rows, TILE), BF16)
    turned = pltpu.VMEM((blocks, TILE, BLK), BF16)
    return pl.pallas_call(
        functools.partial(finish_kernel, blocks, chans // TILE),
        out_shape=(nat, nat, nat, nat, jax.ShapeDtypeStruct(total.shape, F32)),
        in_specs=[anywhere] * 7 + [hbm] * 4,
        out_specs=(hbm,) * 5,
        scratch_shapes=[pltpu.SMEM(docs.shape, jnp.int32), pltpu.VMEM(docs.shape, jnp.int32), pltpu.VMEM(filters.shape, BF16),
                        pltpu.VMEM(total.shape, F32), pltpu.VMEM(total.shape, F32), pltpu.SemaphoreType.DMA((5,))] + [cell] * 8 + [turned] * 4 + [pltpu.VMEM((8 * per, BLK), F32),
                                                    pltpu.SemaphoreType.DMA((4, 2)), pltpu.SemaphoreType.DMA((8,))],
        compiler_params=pltpu.CompilerParams(vmem_limit_bytes=FINISH_VMEM),
        name="finish",
    )(docs, filters, total, *grads, q, k, v, c)


def local(queries, key_inputs, value_inputs, filters, doc_ids, cotangent):
    rows, chans = queries.shape
    groups, taps = filters.shape
    count, wide = lax.axis_size("seq"), lax.axis_size("tp")
    docs = doc_ids.reshape(rows // BLK, BLK)
    bank = filters.reshape(1, groups, taps)
    bound = 1.5 * math.sqrt(groups * wide * taps * (chans // groups) * rows * count)
    *grads, total = fused_call(count, wide, bound, queries, key_inputs, value_inputs, cotangent, bank, docs)
    return finish_call(grads, total, queries, key_inputs, value_inputs, cotangent, bank, docs)


def solution(mesh):
    cells, bank = P("seq", "tp"), P("tp", None)
    return jax.shard_map(local, mesh=mesh, in_specs=(cells, cells, cells, bank, P("seq"), cells),
                         out_specs=(cells, cells, cells, cells, bank), check_vma=False)
```
